512 devices in a mesh: batch: 16 (over y, x_lo), feat: 32 (over z, x_hi, core).
Axes of the slice: x: 4 (x_hi: 2, x_lo: 2; x = x_hi * 2 + x_lo), y: 8, z: 8, core: 2. Of those that a mesh axis runs over, the one named last changes fastest.
Arguments:
- view_a: bfloat16 [8192, 4096], P('batch', 'feat')
- view_b: bfloat16 [8192, 4096], P('batch', 'feat')
Outputs:
- grad_a: bfloat16 [8192, 4096], P('batch', 'feat')
- grad_b: bfloat16 [8192, 4096], P('batch', 'feat')
- correlation: float32 [4096, 4096], P('feat', 'batch')
All inputs are finite; a program needn't handle non-finite values.
Results may differ from the reference program's by a relative error of at most 0.0065.
Values may be sent and summed in bfloat16 or wider, within the bound.
A program may use at most 64 MiB of HBM per device.

```python
import jax
import jax.numpy as jnp
from jax import lax

D = 4096
BATCH = 8192


def blended(key, shape):
    keys = jax.random.split(key, 1)
    gauss = jax.random.normal(keys[0], shape, jnp.float32)
    return gauss


def common_part(key, spread):
    keys = jax.random.split(key, 4)
    own_part = blended(keys[0], (BATCH, D))
    factor = blended(keys[1], (BATCH, 8))
    members = jax.random.randint(keys[2], (D,), 0, 8)
    shared = own_part + factor[:, members]
    ramp_pos = jnp.arange(BATCH, dtype=jnp.float32) / BATCH
    row_scale = 3.0 ** ramp_pos * spread ** jax.random.uniform(keys[3], (BATCH,), jnp.float32)
    return (shared, row_scale)


def view_from(key, shared, row_scale):
    keys = jax.random.split(key, 3)
    view_noise = blended(keys[0], (BATCH, D))
    col_scale = 10.0 ** jax.random.uniform(keys[1], (D,), jnp.float32)
    col_shift = jax.random.uniform(keys[2], (D,), jnp.float32, -1.0, 1.0) * col_scale
    values = col_scale * (row_scale[:, None] * (shared + 0.8 * view_noise)) + col_shift
    return values.astype(jnp.bfloat16)


def draw_view_a(key, part):
    spread = 10.0
    shared, row_scale = common_part(key, spread)
    key = jax.random.fold_in(key, 11)
    return view_from(key, shared, row_scale)


def draw_view_b(key, part):
    spread = 10.0
    shared, row_scale = common_part(key, spread)
    key = jax.random.fold_in(key, 12)
    return view_from(key, shared, row_scale)


def setup_inputs(seed: int = 0) -> dict:
    key_list = jax.random.split(jax.random.key(seed), 3)
    view_a = draw_view_a(jax.random.fold_in(key_list[2], 71), 0)
    view_b = draw_view_b(jax.random.fold_in(key_list[2], 71), 0)
    return dict(view_a=view_a, view_b=view_b)


epsilon = 1e-05
off_weight = 0.0051

def normalize(view):
    wide = view.astype(jnp.float32)
    mean_v = lax.optimization_barrier(jnp.sum(wide, axis=0)) / BATCH
    second = lax.optimization_barrier(jnp.sum(wide * wide, axis=0)) / BATCH
    inverse = lax.rsqrt(second - mean_v * mean_v + epsilon)
    return (((wide - mean_v) * inverse).astype(jnp.bfloat16), inverse)

def finish(back, normed, inverse):
    wide_norm = normed.astype(jnp.float32)
    projected = lax.optimization_barrier(jnp.sum(back * wide_norm, axis=0)) / BATCH
    return (inverse * (back - wide_norm * projected)).astype(jnp.bfloat16)

def reference(view_a, view_b):
    norm_a, inv_a = normalize(view_a)
    norm_b, inv_b = normalize(view_b)
    correlation = jnp.dot(norm_a.T, norm_b, preferred_element_type=jnp.float32) / BATCH
    on_diag = jnp.arange(D)[:, None] == jnp.arange(D)[None, :]
    grad_corr = jnp.where(on_diag, -2.0 * (1.0 - correlation), 2.0 * off_weight * correlation).astype(jnp.bfloat16)
    back_a = jnp.dot(norm_b, grad_corr.T, preferred_element_type=jnp.float32)
    back_b = jnp.dot(norm_a, grad_corr, preferred_element_type=jnp.float32)
    return (finish(back_a, norm_a, inv_a), finish(back_b, norm_b, inv_b), correlation)
```

```python
import jax
import jax.numpy as jnp
from jax import lax
from jax.experimental import pallas as pl
from jax.experimental.pallas import tpu as pltpu
from jax.sharding import PartitionSpec as P

MESH = pl.DeviceIdType.MESH
epsilon = 1e-05
off_weight = 0.0051
f32 = jnp.float32
bf16 = jnp.bfloat16


def div(a, n):
    return lax.div(a, jnp.int32(n))


def rem(a, n):
    return lax.rem(a, jnp.int32(n))


def kernel(
    pairs,
    va, vb,
    ga, gb, co,
    stat_own, stats, abuf, bbuf, cpart, csend, crecv, ctile, corrb,
    gbuf, pbuf, asend, bsend, aback, bback,
    bar_unused,
    st_s, st_r, a_s, a_r, b_s, b_r, c_s, c_r, o_s, o_r, g_s, g_r, p_s, p_r, fa_s, fa_r, fb_s, fb_r,
):
    b = lax.axis_index("batch")
    f = lax.axis_index("feat")
    y, l = div(b, 2), rem(b, 2)
    z, h, c = div(f, 4), rem(div(f, 2), 2), rem(f, 2)
    xi = l * 4 + h * 2 + c

    def dev(y_, z_, h_, l_, c_):
        return (y_ * 2 + l_, z_ * 4 + h_ * 2 + c_)

    def ring_dev(y_, z_, xi_):
        return dev(y_, z_, rem(div(xi_, 2), 2), div(xi_, 4), rem(xi_, 2))

    def send(src, dst, s_sem, r_sem, to):
        pltpu.make_async_remote_copy(
            src_ref=src, dst_ref=dst, send_sem=s_sem, recv_sem=r_sem, device_id=to, device_id_type=MESH
        ).start()

    def wait(ref, sem):
        pltpu.make_async_copy(ref, ref, sem).wait()

    def loop(lo, hi, fn):
        def step(i, carry):
            fn(i)
            return carry

        lax.fori_loop(lo, hi, step, 0)

    barrier = pltpu.get_barrier_semaphore()

    def greet(to):
        pl.semaphore_signal(barrier, inc=1, device_id=to, device_id_type=MESH)

    loop(1, 16, lambda e: greet((rem(b + e, 16), f)))
    loop(1, 8, lambda e: greet(ring_dev(y, z, rem(xi + e, 8))))
    loop(1, 8, lambda e: greet(dev(y, rem(z + e, 8), h, l, c)))
    loop(1, 8, lambda e: greet(dev(y, rem(z + e, 8), h, 1 - l, c)))
    y_near = div(y, 2) * 2 + 1 - rem(y, 2)
    loop(0, 8, lambda e: greet(ring_dev(y_near, z, rem(xi + e, 8))))

    wide_a = va[...].astype(f32)
    wide_b = vb[...].astype(f32)
    stat_own[0:1, :] = jnp.sum(wide_a, axis=0, keepdims=True)
    stat_own[1:2, :] = jnp.sum(wide_a * wide_a, axis=0, keepdims=True)
    stat_own[2:3, :] = jnp.sum(wide_b, axis=0, keepdims=True)
    stat_own[3:4, :] = jnp.sum(wide_b * wide_b, axis=0, keepdims=True)
    stat_own[4:8, :] = jnp.zeros((4, 128), f32)
    stats[b] = stat_own[...]

    pl.semaphore_wait(barrier, 15 + 7 + 7 + 7 + 8)

    loop(1, 16, lambda e: send(stat_own, stats.at[b], st_s.at[e], st_r.at[b], (rem(b + e, 16), f)))
    loop(1, 16, lambda e: wait(stats.at[rem(b + e, 16)], st_r.at[rem(b + e, 16)]))
    total = stats[0]
    for i in range(1, 16):
        total = total + stats[i]
    total = total / pairs
    mean_a, mean_b = total[0:1, :], total[2:3, :]
    inv_a = lax.rsqrt(total[1:2, :] - mean_a * mean_a + epsilon)
    inv_b = lax.rsqrt(total[3:4, :] - mean_b * mean_b + epsilon)

    half = rem(z, 2)
    bslot = l * 4 + div(z, 2)
    bbuf[8] = ((vb[...].astype(f32) - mean_b) * inv_b).astype(bf16)
    loop(1, 8, lambda e: send(bbuf.at[8], bbuf.at[bslot], b_s.at[e], b_r.at[bslot], dev(y, rem(z + e, 8), h, half, c)))

    @pl.when(half != l)
    def _():
        send(bbuf.at[8], bbuf.at[bslot], b_s.at[0], b_r.at[bslot], dev(y, z, h, half, c))

    abuf[xi] = ((va[...].astype(f32) - mean_a) * inv_a).astype(bf16)
    loop(
        1, 8,
        lambda e: send(abuf.at[xi], abuf.at[xi], a_s.at[e], a_r.at[xi], ring_dev(y, z, rem(xi + e, 8))),
    )

    @pl.when(half == l)
    def _():
        bbuf[bslot] = bbuf[8]

    loop(1, 8, lambda e: wait(abuf.at[rem(xi + e, 8)], a_r.at[rem(xi + e, 8)]))
    loop(1, 8, lambda e: wait(bbuf.at[rem(bslot + e, 8)], b_r.at[rem(bslot + e, 8)]))

    @pl.when(half != l)
    def _():
        wait(bbuf.at[bslot], b_r.at[bslot])

    def side(buf, k):
        return jnp.concatenate([buf[k * 4 + i] for i in range(4)], axis=1)

    over_rows = (((0,), (0,)), ((), ()))
    over_cols = (((1,), (1,)), ((), ()))
    over_in = (((1,), (0,)), ((), ()))
    whole_a = jnp.concatenate([side(abuf, 0), side(abuf, 1)], axis=0)
    whole_b = jnp.concatenate([side(bbuf, 0), side(bbuf, 1)], axis=0)
    prod = lax.dot_general(whole_a, whole_b, over_rows, preferred_element_type=f32)
    for q in range(4):
        cpart[q] = prod[:, q * 128 : (q + 1) * 128]
    for q in range(4):
        for s in range(2):
            flip = l if s == 0 else 1 - l
            csend[2 * q + flip] = cpart[q, s * 256 : (s + 1) * 256, :].astype(bf16)

    loop(
        1, 8,
        lambda e: send(
            csend.at[rem(y + e, 8)], crecv.at[y], c_s.at[e], c_r.at[y], dev(rem(y + e, 8), z, h, l, c)
        ),
    )
    mine = rem(rem(y, 2) + l, 2)
    q_own = div(y, 2)
    ctile[...] = cpart[q_own, pl.ds(pl.multiple_of(mine * 256, 256), 256), :]
    def add(e):
        frm = rem(y + e, 8)
        wait(crecv.at[frm], c_r.at[frm])
        ctile[...] += crecv[frm].astype(f32)

    loop(1, 8, add)
    corr = ctile[...] / pairs
    ctile[...] = corr

    row_ids = lax.broadcasted_iota(jnp.int32, corr.shape, 0)
    col_ids = lax.broadcasted_iota(jnp.int32, corr.shape, 1)
    here = jnp.where((z == 2 * q_own + l) & (mine == h), c * 128, -100000)
    grad = jnp.where(row_ids == col_ids + here, -2.0 * (1.0 - corr), 2.0 * off_weight * corr).astype(bf16)
    gbuf[y] = grad
    loop(
        1, 8,
        lambda e: send(gbuf.at[y], gbuf.at[y], g_s.at[e], g_r.at[y], dev(rem(y + e, 8), z, h, l, c)),
    )
    both = grad.astype(f32) * corr
    flipped = jnp.sum(both.T, axis=0, keepdims=True)
    pbuf[y, 0:1, :] = jnp.sum(both, axis=0, keepdims=True)
    pbuf[y, 1:2, :] = flipped[:, :128]
    pbuf[y, 2:3, :] = flipped[:, 128:]
    pbuf[y, 3:8, :] = jnp.zeros((5, 128), f32)
    loop(
        1, 8,
        lambda e: send(pbuf.at[y], pbuf.at[y], p_s.at[e], p_r.at[y], dev(rem(y + e, 8), z, h, l, c)),
    )

    y_out = 2 * q_own + l
    at_home = (y_out == y) & (mine == h) & (h == l)
    for k in range(2):
        stay = at_home & (c == k)

        @pl.when(stay)
        def _(k=k):
            corrb[c] = ctile[k * 128 : (k + 1) * 128, :]

        @pl.when(jnp.logical_not(stay))
        def _(k=k):
            send(
                ctile.at[pl.ds(k * 128, 128)], corrb.at[c], o_s.at[k], o_r.at[c], dev(y_out, z, mine, h, jnp.int32(k))
            )

    loop(1, 8, lambda e: wait(gbuf.at[rem(y + e, 8)], g_r.at[rem(y + e, 8)]))
    loop(1, 8, lambda e: wait(pbuf.at[rem(y + e, 8)], p_r.at[rem(y + e, 8)]))

    def grad_cols(q):
        return jnp.concatenate([gbuf[2 * q + l], gbuf[2 * q + 1 - l]], axis=0)

    whole_g = jnp.concatenate([grad_cols(q) for q in range(4)], axis=1)
    proj_b = [pbuf[2 * q, 0:1, :] + pbuf[2 * q + 1, 0:1, :] for q in range(4)]
    proj_a = []
    for i in range(4):
        flip = l if i < 2 else 1 - l
        r = 1 + i % 2
        proj_a.append(sum(pbuf[2 * q + flip, r : r + 1, :] for q in range(4)))

    for k in range(2):
        back = lax.dot_general(side(abuf, k), whole_g, over_in, preferred_element_type=f32)
        for q in range(4):
            bsend[k * 4 + q] = (back[:, q * 128 : (q + 1) * 128] - bbuf[k * 4 + q].astype(f32) * proj_b[q]).astype(bf16)
            to_z = 2 * q + l
            stay = (to_z == z) & (l == k)

            @pl.when(stay)
            def _(k=k, q=q):
                bback[z] = bsend[k * 4 + q]

            @pl.when(jnp.logical_not(stay))
            def _(k=k, q=q, to_z=to_z):
                send(
                    bsend.at[k * 4 + q], bback.at[z], fb_s.at[k * 4 + q], fb_r.at[z], dev(y, to_z, h, jnp.int32(k), c)
                )
    for k in range(2):
        back = lax.dot_general(side(bbuf, k), whole_g, over_cols, preferred_element_type=f32)
        for i in range(4):
            asend[k * 4 + i] = (back[:, i * 128 : (i + 1) * 128] - abuf[k * 4 + i].astype(f32) * proj_a[i]).astype(bf16)
    aback[xi] = asend[xi]
    loop(
        1, 8,
        lambda e: send(
            asend.at[rem(xi + e, 8)], aback.at[xi], fa_s.at[e], fa_r.at[xi], ring_dev(y, z, rem(xi + e, 8))
        ),
    )

    c_from = jnp.where((rem(y, 2) == l) & (h == 0), 1, 0)
    for k in range(2):
        own = (h == l) & (rem(y, 2) == l) & (rem(rem(y, 2) + l, 2) == h) & (c == k)

        @pl.when(jnp.logical_not(own))
        def _(k=k):
            wait(corrb.at[k], o_r.at[k])

        co[:, k * 128 : (k + 1) * 128] = corrb[k]
    del c_from

    loop(1, 8, lambda e: wait(aback.at[rem(xi + e, 8)], fa_r.at[rem(xi + e, 8)]))
    acc = aback[0].astype(f32)
    for i in range(1, 8):
        acc = acc + aback[i].astype(f32)
    ga[...] = (acc * inv_a).astype(bf16)
    loop(1, 8, lambda e: wait(bback.at[rem(z + e, 8)], fb_r.at[rem(z + e, 8)]))

    @pl.when(half != l)
    def _():
        wait(bback.at[z], fb_r.at[z])

    acc = bback[0].astype(f32)
    for i in range(1, 8):
        acc = acc + bback[i].astype(f32)
    gb[...] = (acc * inv_b).astype(bf16)

    loop(1, 16, lambda e: wait(stat_own, st_s.at[e]))
    loop(1, 8, lambda e: wait(bbuf.at[8], b_s.at[e]))

    @pl.when(half != l)
    def _():
        wait(bbuf.at[8], b_s.at[0])

    loop(1, 8, lambda e: wait(abuf.at[xi], a_s.at[e]))
    loop(1, 8, lambda e: wait(csend.at[rem(y + e, 8)], c_s.at[e]))
    loop(1, 8, lambda e: wait(gbuf.at[y], g_s.at[e]))
    loop(1, 8, lambda e: wait(pbuf.at[y], p_s.at[e]))
    loop(1, 8, lambda e: wait(asend.at[rem(xi + e, 8)], fa_s.at[e]))
    for k in range(2):
        @pl.when(jnp.logical_not(at_home & (c == k)))
        def _(k=k):
            wait(ctile.at[pl.ds(k * 128, 128)], o_s.at[k])

        for q in range(4):
            @pl.when(jnp.logical_not((2 * q + l == z) & (l == k)))
            def _(k=k, q=q):
                wait(bsend.at[k * 4 + q], fb_s.at[k * 4 + q])


def body(view_a, view_b):
    rows, cols = view_a.shape
    pairs = rows * lax.axis_size("batch")
    vmem = pl.BlockSpec(memory_space=pltpu.VMEM)
    dma = pltpu.SemaphoreType.DMA

    def call(*args):
        return kernel(float(pairs), *args)

    return pl.pallas_call(
        call,
        name="barlow",
        out_shape=(
            jax.ShapeDtypeStruct((rows, cols), bf16),
            jax.ShapeDtypeStruct((rows, cols), bf16),
            jax.ShapeDtypeStruct((128, 256), f32),
        ),
        in_specs=[vmem, vmem],
        out_specs=(vmem, vmem, vmem),
        scratch_shapes=[
            pltpu.VMEM((8, 128), f32),
            pltpu.VMEM((16, 8, 128), f32),
            pltpu.VMEM((8, rows, 128), bf16),
            pltpu.VMEM((9, rows, 128), bf16),
            pltpu.VMEM((4, 512, 128), f32),
            pltpu.VMEM((8, 256, 128), bf16),
            pltpu.VMEM((8, 256, 128), bf16),
            pltpu.VMEM((256, 128), f32),
            pltpu.VMEM((2, 128, 128), f32),
            pltpu.VMEM((8, 256, 128), bf16),
            pltpu.VMEM((8, 8, 128), f32),
            pltpu.VMEM((8, rows, 128), bf16),
            pltpu.VMEM((8, rows, 128), bf16),
            pltpu.VMEM((8, rows, 128), bf16),
            pltpu.VMEM((8, rows, 128), bf16),
            pltpu.SemaphoreType.REGULAR,
            dma((16,)), dma((16,)),
            dma((8,)), dma((8,)), dma((8,)), dma((8,)), dma((8,)), dma((8,)),
            dma((2,)), dma((2,)), dma((8,)), dma((8,)), dma((8,)), dma((8,)),
            dma((8,)), dma((8,)), dma((8,)), dma((8,)),
        ],
        compiler_params=pltpu.CompilerParams(
            collective_id=0, has_side_effects=True, vmem_limit_bytes=40 * 2**20
        ),
    )(view_a, view_b)


def solution(mesh):
    return jax.shard_map(
        body,
        mesh=mesh,
        in_specs=(P("batch", "feat"), P("batch", "feat")),
        out_specs=(P("batch", "feat"), P("batch", "feat"), P("feat", "batch")),
        check_vma=False,
    )
```

```python
import jax
import jax.numpy as jnp
from jax import lax
from jax.experimental import pallas as pl
from jax.experimental.pallas import tpu as pltpu
from jax.sharding import PartitionSpec as P

MESH = pl.DeviceIdType.MESH
epsilon = 1e-05
off_weight = 0.0051
f32 = jnp.float32
bf16 = jnp.bfloat16


def div(a, n):
    return lax.div(a, jnp.int32(n))


def rem(a, n):
    return lax.rem(a, jnp.int32(n))


def kernel(
    pairs,
    va, vb,
    ga, gb, co,
    stat_own, stats, abuf, bbuf, aturn, cwide, cnarrow, crecv, cpass, ctile, corrb,
    gbuf, gfull, bsend, bkeep, bfull, bhalf, bpass, bback, asend, akeep, ain, apass, aback,
    st_s, st_r, a_s, a_r, b_s, b_r, bp_s, c_s, cp_s, cp_r, c_r, o_s, o_r, g_s, gp_r, g_r,
    fb_s, fbp_s, ff_r, fh_r, fb_r, fd_s, fd_r, fa_s, fa_r,
):
    b = lax.axis_index("batch")
    f = lax.axis_index("feat")
    y, l = div(b, 2), rem(b, 2)
    z, h, c = div(f, 4), rem(div(f, 2), 2), rem(f, 2)
    xi = l * 4 + h * 2 + c

    def dev(y_, z_, h_, l_, c_):
        return (y_ * 2 + l_, z_ * 4 + h_ * 2 + c_)

    def ring_dev(y_, z_, xi_):
        return dev(y_, z_, rem(div(xi_, 2), 2), div(xi_, 4), rem(xi_, 2))

    def send(src, dst, s_sem, r_sem, to):
        pltpu.make_async_remote_copy(
            src_ref=src, dst_ref=dst, send_sem=s_sem, recv_sem=r_sem, device_id=to, device_id_type=MESH
        ).start()

    def wait(ref, sem):
        pltpu.make_async_copy(ref, ref, sem).wait()

    def loop(lo, hi, fn):
        def step(i, carry):
            fn(i)
            return carry

        lax.fori_loop(lo, hi, step, 0)

    def corr_to(q):
        return dev(2 * q + l, z, div(y, 4), h, rem(div(y, 2), 2))

    def corr_from(k, p):
        return dev(h * 4 + c * 2 + p, z, l, rem(y, 2), k)

    at_home = (rem(y, 2) == l) & (h == l) & (div(y, 2) == h * 2 + c)

    barrier = pltpu.get_barrier_semaphore()

    def greet(to):
        pl.semaphore_signal(barrier, inc=1, device_id=to, device_id_type=MESH)

    loop(1, 16, lambda e: greet((rem(b + e, 16), f)))
    loop(1, 8, lambda e: greet(ring_dev(y, z, rem(xi + e, 8))))
    loop(1, 8, lambda e: greet(dev(y, rem(z + e, 8), h, l, c)))
    loop(1, 8, lambda e: greet(dev(y, rem(z + e, 8), h, 1 - l, c)))
    for q in range(4):
        @pl.when(jnp.logical_not(at_home & (div(y, 2) == q)))
        def _(q=q):
            greet(corr_to(q))

        @pl.when(jnp.logical_not(at_home & (c == q // 2) & (rem(y, 2) == q % 2)))
        def _(q=q):
            greet(corr_from(q // 2, q % 2))

    wide_a = va[...].astype(f32)
    wide_b = vb[...].astype(f32)
    stat_own[0:1, :] = jnp.sum(wide_a, axis=0, keepdims=True)
    stat_own[1:2, :] = jnp.sum(wide_a * wide_a, axis=0, keepdims=True)
    stat_own[2:3, :] = jnp.sum(wide_b, axis=0, keepdims=True)
    stat_own[3:4, :] = jnp.sum(wide_b * wide_b, axis=0, keepdims=True)
    stat_own[4:8, :] = jnp.zeros((4, 128), f32)
    stats[b] = stat_own[...]

    pl.semaphore_wait(barrier, 15 + 7 + 7 + 7 + 8 - 2 * at_home.astype(jnp.int32))

    loop(1, 16, lambda e: send(stat_own, stats.at[b], st_s, st_r, (rem(b + e, 16), f)))
    wait(stats.at[pl.ds(0, 15)], st_r)
    total = stats[0]
    for i in range(1, 16):
        total = total + stats[i]
    total = total / pairs
    mean_a, mean_b = total[0:1, :], total[2:3, :]
    inv_a = lax.rsqrt(total[1:2, :] - mean_a * mean_a + epsilon)
    inv_b = lax.rsqrt(total[3:4, :] - mean_b * mean_b + epsilon)

    half = rem(z, 2)
    native = half == l
    bslot = l * 4 + div(z, 2)
    bbuf[8] = ((vb[...].astype(f32) - mean_b) * inv_b).astype(bf16)
    for i, d in enumerate((2, 6, 1, 7)):
        send(bbuf.at[8], bbuf.at[bslot], b_s.at[i], b_r.at[bslot], dev(y, rem(z + d, 8), h, half, c))
    abuf[xi] = ((va[...].astype(f32) - mean_a) * inv_a).astype(bf16)
    twin = xi + 1 - 2 * c
    for i, e in enumerate((4, 2, 6)):
        send(abuf.at[xi], abuf.at[xi], a_s.at[i], a_r.at[xi], ring_dev(y, z, rem(xi + e, 8)))
    send(abuf.at[xi], abuf.at[xi], a_s.at[3], a_r.at[xi], ring_dev(y, z, twin))

    @pl.when(jnp.logical_not(native))
    def _():
        send(bbuf.at[8], bbuf.at[bslot], b_s.at[4], b_r.at[bslot], dev(y, z, h, half, c))

    @pl.when(native)
    def _():
        bbuf[bslot] = bbuf[8]
        for p, (frm, one, two) in enumerate(((6, 1, 2), (2, 7, 6))):
            for k in range(2):
                slot = k * 4 + div(rem(z + frm, 8), 2)
                wait(bbuf.at[slot], b_r.at[slot])
                send(bbuf.at[slot], bbuf.at[slot], bp_s.at[p, k, 0], b_r.at[slot], dev(y, rem(z + one, 8), h, l, c))
                part = bbuf.at[slot, pl.ds(p * 256, 256)]
                send(part, part, bp_s.at[p, k, 1], b_r.at[slot], dev(y, rem(z + two, 8), h, l, c))

    def turn(slot):
        aturn[rem(slot, 4), :, pl.ds(pl.multiple_of(div(slot, 4) * 512, 512), 512)] = abuf[slot].T

    turn(xi)
    for i, e in enumerate((2, 6, 4)):
        slot = rem(xi + e, 8)
        wait(abuf.at[slot], a_r.at[slot])
        send(abuf.at[slot], abuf.at[slot], a_s.at[4 + i], a_r.at[slot], ring_dev(y, z, twin))
        turn(slot)
    for e in (0, 2, 6, 4):
        slot = rem(twin + e, 8)
        wait(abuf.at[slot], a_r.at[slot])
        turn(slot)

    def side(buf, k):
        return jnp.concatenate([buf[k * 4 + i] for i in range(4)], axis=1)

    over_cols = (((1,), (1,)), ((), ()))
    over_in = (((1,), (0,)), ((), ()))

    def block(t):
        ahead = jnp.where(native, (2, 6, 4, 0)[t], (3, 5, 1, 7)[t])
        return div(rem(z + ahead, 8), 2)

    def along_y(e):
        return dev(rem(y + e, 8), z, h, l, c)

    def rows_of(to):
        return pl.ds(pl.multiple_of(to * 64, 64), 64)

    def correlate(t):
        q = block(t)
        for k in range(2):
            if t < 2:
                @pl.when(jnp.logical_not(native))
                def _(k=k):
                    wait(bbuf.at[k * 4 + q], b_r.at[k * 4 + q])
            elif t == 2:
                wait(bbuf.at[k * 4 + q], b_r.at[k * 4 + q])
            else:
                @pl.when(jnp.logical_not(native & (l == k)))
                def _(k=k):
                    wait(bbuf.at[k * 4 + q], b_r.at[k * 4 + q])

        right = jnp.concatenate([bbuf[q], bbuf[4 + q]], axis=0)
        left = jnp.concatenate([aturn[i] for i in range(4)], axis=0)
        part = lax.dot_general(left, right, over_in, preferred_element_type=f32)
        cwide[t] = part
        cnarrow[t] = part.astype(bf16)

        def go(e, to, slot, sem, lo=0, n=64):
            piece = cnarrow.at[t, pl.ds(pl.multiple_of(rem(y + e, 8) * 64 + lo, 32), n)]
            send(piece, crecv.at[t, slot, pl.ds(lo, n)], c_s.at[t], sem, along_y(to))

        go(3, 1, 2, cp_r.at[t])
        go(5, 7, 3, cp_r.at[t])
        go(4, 6, 4, cp_r.at[t], 0, 32)
        go(4, 2, 5, cp_r.at[t], 32, 32)
        go(1, 1, 0, c_r.at[t])
        go(7, 7, 1, c_r.at[t])

    def pass_partial(t):
        wait(crecv.at[t, pl.ds(0, 3)], cp_r.at[t])
        up = cwide[t, rows_of(rem(y + 2, 8)), :] + crecv[t, 2].astype(f32)
        cpass[t, 0, 0:32, :] = up[:32].astype(bf16)
        cpass[t, 0, 32:64, :] = (up[32:] + crecv[t, 5, 32:64, :].astype(f32)).astype(bf16)
        send(cpass.at[t, 0], crecv.at[t, 6], cp_s.at[t], c_r.at[t], along_y(2))
        down = cwide[t, rows_of(rem(y + 6, 8)), :] + crecv[t, 3].astype(f32)
        cpass[t, 1, 0:32, :] = (down[:32] + crecv[t, 4, 0:32, :].astype(f32)).astype(bf16)
        cpass[t, 1, 32:64, :] = down[32:].astype(bf16)
        send(cpass.at[t, 1], crecv.at[t, 7], cp_s.at[t], c_r.at[t], along_y(6))

    def differentiate(t):
        q = block(t)
        wait(crecv.at[t, pl.ds(0, 4)], c_r.at[t])
        corr = cwide[t, rows_of(y), :]
        for i in (0, 1, 6, 7):
            corr = corr + crecv[t, i].astype(f32)
        corr = corr / pairs
        ctile[q] = corr
        row_ids = lax.broadcasted_iota(jnp.int32, corr.shape, 0)
        col_ids = lax.broadcasted_iota(jnp.int32, corr.shape, 1)
        here = jnp.where((z == 2 * q + l) & (div(y, 2) == h * 2 + c), rem(y, 2) * 64, 100000)
        grad = jnp.where(row_ids + here == col_ids, -2.0 * (1.0 - corr), 2.0 * off_weight * corr).astype(bf16)
        both = grad.astype(f32) * corr
        cols = jnp.sum(both, axis=0, keepdims=True)
        rows = jnp.sum(both.T, axis=0, keepdims=True)
        none = jnp.zeros_like(rows)
        rows = jnp.where(
            rem(y, 2) == 0, jnp.concatenate([rows, none], axis=1), jnp.concatenate([none, rows], axis=1)
        )
        terms = []
        for value in (cols, rows):
            high = value.astype(bf16).astype(f32)
            terms += [high, value - high]
        terms.append(jnp.zeros((12, 128), f32))
        gbuf[q, y, 0:64, :] = grad
        gbuf[q, y, 64:80, :] = jnp.concatenate(terms, axis=0).astype(bf16)
        send(gbuf.at[q, y], gbuf.at[q, y], g_s.at[t], gp_r.at[t], along_y(2))
        send(gbuf.at[q, y], gbuf.at[q, y], g_s.at[t], gp_r.at[t], along_y(6))
        send(gbuf.at[q, y], gbuf.at[q, y], g_s.at[t], g_r.at[t], along_y(1))
        send(gbuf.at[q, y], gbuf.at[q, y], g_s.at[t], g_r.at[t], along_y(7))

    def pass_gradient(t):
        q = block(t)
        wait(gbuf.at[q, pl.ds(0, 2)], gp_r.at[t])
        for frm, one, two, lo, n in ((6, 1, 2, 0, 48), (2, 7, 6, 48, 32)):
            item = gbuf.at[q, rem(y + frm, 8)]
            send(item, item, g_s.at[t], g_r.at[t], along_y(one))
            part = gbuf.at[q, rem(y + frm, 8), pl.ds(lo, n)]
            send(part, part, g_s.at[t], g_r.at[t], along_y(two))

    proj_a = [jnp.zeros((1, 128), f32)] * 4
    proj_b = []

    def take_gradient(t):
        q = block(t)
        wait(gbuf.at[q, pl.ds(0, 5)], g_r.at[t])
        total = jnp.zeros((1, 128), f32)
        for i in range(8):
            gfull[q, i * 64 : (i + 1) * 64, :] = gbuf[q, i, 0:64, :]
            sums = gbuf[q, i, 64:80, :].astype(f32)
            total = total + (sums[0:1, :] + sums[1:2, :])
            proj_a[i // 2] = proj_a[i // 2] + (sums[2:3, :] + sums[3:4, :])
        proj_b.append(total)

    def in_column(d):
        return dev(y, rem(z + d, 8), h, l, c)

    def back_columns(t):
        q = block(t)
        for k in range(2):
            back = lax.dot_general(side(abuf, k), gfull[q], over_in, preferred_element_type=f32)
            back = back - bbuf[k * 4 + q].astype(f32) * proj_b[t]
            if t < 2:
                bkeep[t, k] = back
            bsend[t, k] = back.astype(bf16)

            if t < 2:
                @pl.when(jnp.logical_not(native))
                def _(k=k):
                    send(bsend.at[t, k], bfull.at[t, k], fb_s.at[t, k], ff_r.at[t, k], in_column((1, 7)[t]))
            elif t == 2:
                @pl.when(native)
                def _(k=k):
                    for p, d in enumerate((2, 6)):
                        rows = pl.ds(256 - p * 256, 256)
                        send(
                            bsend.at[t, k, rows], bhalf.at[p, k, rows], fb_s.at[t, k], fh_r.at[p, k], in_column(d)
                        )

                @pl.when(jnp.logical_not(native))
                def _(k=k):
                    send(
                        bsend.at[t, k], bback.at[0], fb_s.at[t, k], fb_r.at[0], dev(y, rem(z + 1, 8), h, jnp.int32(k), c)
                    )
            else:
                @pl.when(native & (l == k))
                def _(k=k):
                    bback[4] = bsend[t, k]

                @pl.when(native & (l != k))
                def _(k=k):
                    send(bsend.at[t, k], bback.at[4], fb_s.at[t, k], fb_r.at[4], dev(y, z, h, jnp.int32(k), c))

                @pl.when(jnp.logical_not(native))
                def _(k=k):
                    send(
                        bsend.at[t, k], bback.at[1], fb_s.at[t, k], fb_r.at[1], dev(y, rem(z + 7, 8), h, jnp.int32(k), c)
                    )

    def pass_back():
        for p, d in enumerate((2, 6)):
            for k in range(2):
                rows = pl.ds(256 - p * 256, 256)
                wait(bfull.at[p, k], ff_r.at[p, k])
                wait(bhalf.at[p, k, rows], fh_r.at[p, k])
                one = slice(256 - p * 256, 512 - p * 256)
                other = slice(p * 256, 256 + p * 256)
                bpass[p, k, other, :] = (bkeep[p, k, other, :] + bfull[p, k, other, :].astype(f32)).astype(bf16)
                bpass[p, k, one, :] = (
                    bkeep[p, k, one, :] + bfull[p, k, one, :].astype(f32) + bhalf[p, k, one, :].astype(f32)
                ).astype(bf16)
                send(
                    bpass.at[p, k], bback.at[2 + p], fbp_s.at[p, k], fb_r.at[2 + p],
                    dev(y, rem(z + d, 8), h, jnp.int32(k), c),
                )

    correlate(0)
    correlate(1)
    pass_partial(0)
    correlate(2)
    pass_partial(1)
    differentiate(0)
    correlate(3)
    pass_partial(2)
    differentiate(1)
    pass_gradient(0)
    pass_partial(3)
    differentiate(2)
    pass_gradient(1)
    take_gradient(0)
    back_columns(0)
    differentiate(3)
    pass_gradient(2)
    take_gradient(1)
    back_columns(1)
    pass_gradient(3)
    take_gradient(2)
    back_columns(2)

    for q in range(4):
        stay = at_home & (div(y, 2) == q)

        @pl.when(stay)
        def _(q=q):
            corrb[c, rem(y, 2)] = ctile[q]

        @pl.when(jnp.logical_not(stay))
        def _(q=q):
            send(ctile.at[q], corrb.at[c, rem(y, 2)], o_s.at[q], o_r.at[c, rem(y, 2)], corr_to(q))

    take_gradient(3)
    whole_g = jnp.concatenate([gfull[q] for q in range(4)], axis=1)
    for k in range(2):
        back = lax.dot_general(side(bbuf, k), whole_g, over_cols, preferred_element_type=f32)
        for i in range(4):
            less = back[:, i * 128 : (i + 1) * 128] - abuf[k * 4 + i].astype(f32) * proj_a[i]
            akeep[k * 4 + i] = less
            asend[k * 4 + i] = less.astype(bf16)
    chip = l * 2 + h
    for e in (2, 1, 3, 0):
        to = rem(chip + e, 4)
        send(asend.at[to * 2 + 1 - c], ain.at[to], fd_s.at[e], fd_r.at[to], ring_dev(y, z, twin))

    back_columns(3)

    for e in (2, 1, 3, 0):
        to = rem(chip + e, 4)
        wait(ain.at[to], fd_r.at[to])
        summed = (akeep[to * 2 + c] + ain[to].astype(f32)).astype(bf16)
        if e:
            apass[e] = summed
            send(apass.at[e], aback.at[chip], fa_s.at[e], fa_r.at[chip], ring_dev(y, z, to * 2 + c))
        else:
            aback[chip] = summed

    @pl.when(native)
    def _():
        pass_back()

    for k in range(2):
        for p in range(2):
            @pl.when(jnp.logical_not(at_home & (c == k) & (rem(y, 2) == p)))
            def _(k=k, p=p):
                wait(corrb.at[k, p], o_r.at[k, p])

            co[p * 64 : (p + 1) * 64, k * 128 : (k + 1) * 128] = corrb[k, p]

    for i in range(4):
        wait(bback.at[i], fb_r.at[i])

    @pl.when(jnp.logical_not(native))
    def _():
        wait(bback.at[4], fb_r.at[4])

    acc = bback[0].astype(f32)
    for i in range(1, 5):
        acc = acc + bback[i].astype(f32)
    gb[...] = (acc * inv_b).astype(bf16)

    for e in range(1, 4):
        frm = rem(chip + e, 4)
        wait(aback.at[frm], fa_r.at[frm])
    acc = aback[0].astype(f32)
    for i in range(1, 4):
        acc = acc + aback[i].astype(f32)
    ga[...] = (acc * inv_a).astype(bf16)

    wait(stats.at[pl.ds(0, 15)], st_s)
    for i in range(4):
        wait(bbuf.at[8], b_s.at[i])
    for i in range(7):
        wait(abuf.at[xi], a_s.at[i])
    for e in range(4):
        wait(asend.at[0], fd_s.at[e])
        if e:
            wait(apass.at[e], fa_s.at[e])

    @pl.when(jnp.logical_not(native))
    def _():
        wait(bbuf.at[8], b_s.at[4])

    @pl.when(native)
    def _():
        for p in range(2):
            for k in range(2):
                wait(bbuf.at[8], bp_s.at[p, k, 0])
                wait(bbuf.at[8, pl.ds(0, 256)], bp_s.at[p, k, 1])
                wait(bpass.at[p, k], fbp_s.at[p, k])

    for t in range(4):
        wait(crecv.at[t, pl.ds(0, 5)], c_s.at[t])
        wait(crecv.at[t, pl.ds(0, 2)], cp_s.at[t])
        wait(gbuf.at[t, pl.ds(0, 7)], g_s.at[t])

        @pl.when(jnp.logical_not(at_home & (div(y, 2) == t)))
        def _(t=t):
            wait(ctile.at[t], o_s.at[t])

        for k in range(2):
            @pl.when((jnp.logical_not(native)) | (t == 2) | ((t == 3) & (l != k)))
            def _(k=k, t=t):
                wait(bsend.at[t, k], fb_s.at[t, k])


def body(view_a, view_b):
    rows, cols = view_a.shape
    pairs = rows * lax.axis_size("batch")
    vmem = pl.BlockSpec(memory_space=pltpu.VMEM)
    dma = pltpu.SemaphoreType.DMA

    def call(*args):
        return kernel(float(pairs), *args)

    return pl.pallas_call(
        call,
        name="barlow",
        out_shape=(
            jax.ShapeDtypeStruct((rows, cols), bf16),
            jax.ShapeDtypeStruct((rows, cols), bf16),
            jax.ShapeDtypeStruct((128, 256), f32),
        ),
        in_specs=[vmem, vmem],
        out_specs=(vmem, vmem, vmem),
        scratch_shapes=[
            pltpu.VMEM((8, 128), f32),
            pltpu.VMEM((16, 8, 128), f32),
            pltpu.VMEM((8, rows, 128), bf16),
            pltpu.VMEM((9, rows, 128), bf16),
            pltpu.VMEM((4, 128, 1024), bf16),
            pltpu.VMEM((4, 512, 128), f32),
            pltpu.VMEM((4, 512, 128), bf16),
            pltpu.VMEM((4, 8, 64, 128), bf16),
            pltpu.VMEM((4, 2, 64, 128), bf16),
            pltpu.VMEM((4, 64, 128), f32),
            pltpu.VMEM((2, 2, 64, 128), f32),
            pltpu.VMEM((4, 8, 80, 128), bf16),
            pltpu.VMEM((4, 512, 128), bf16),
            pltpu.VMEM((4, 2, rows, 128), bf16),
            pltpu.VMEM((2, 2, rows, 128), f32),
            pltpu.VMEM((2, 2, rows, 128), bf16),
            pltpu.VMEM((2, 2, rows, 128), bf16),
            pltpu.VMEM((2, 2, rows, 128), bf16),
            pltpu.VMEM((5, rows, 128), bf16),
            pltpu.VMEM((8, rows, 128), bf16),
            pltpu.VMEM((8, rows, 128), f32),
            pltpu.VMEM((4, rows, 128), bf16),
            pltpu.VMEM((4, rows, 128), bf16),
            pltpu.VMEM((4, rows, 128), bf16),
            dma, dma,
            dma((7,)), dma((8,)), dma((5,)), dma((8,)), dma((2, 2, 2)),
            dma((4,)), dma((4,)), dma((4,)), dma((4,)), dma((4,)), dma((2, 2)), dma((4,)), dma((4,)), dma((4,)),
            dma((4, 2)), dma((2, 2)), dma((2, 2)), dma((2, 2)), dma((5,)),
            dma((4,)), dma((4,)), dma((4,)), dma((4,)),
        ],
        compiler_params=pltpu.CompilerParams(
            collective_id=0, has_side_effects=True, vmem_limit_bytes=40 * 2**20
        ),
    )(view_a, view_b)


def solution(mesh):
    return jax.shard_map(
        body,
        mesh=mesh,
        in_specs=(P("batch", "feat"), P("batch", "feat")),
        out_specs=(P("batch", "feat"), P("batch", "feat"), P("feat", "batch")),
        check_vma=False,
    )
```

```python
import jax
import jax.numpy as jnp
from jax import lax
from jax.experimental import pallas as pl
from jax.experimental.pallas import tpu as pltpu
from jax.sharding import PartitionSpec as P

MESH = pl.DeviceIdType.MESH
epsilon = 1e-05
off_weight = 0.0051
f32 = jnp.float32
bf16 = jnp.bfloat16


def div(a, n):
    return lax.div(a, jnp.int32(n))


def rem(a, n):
    return lax.rem(a, jnp.int32(n))


offs_on = ((0, 1), (2, 3), (4, 5), (6, 7))
offs_off = ((7, 0), (5, 6), (3, 4), (1, 2))


def kernel(
    pairs,
    va, vb,
    ga, gb, co,
    stat_own, stats, astat, bstat, abuf, bbuf, anorm, bnorm, aturn, cwide, cnarrow, crecv, cpass, ctile, corrb,
    gbuf, gfull, bsend, bkeep, bfull, bhalf, bpass, bback, bown, bcross, asend, akeep, ain, apass, aback,
    st_s, st_r, ms_s, as_r, bs_r, a_s, a_r, b_s, b_r, bp_s, c_s, cp_s, cp_r, c_r, o_s, o_r, g_s, gp_r, g_r,
    fb_s, fbp_s, ff_r, fh_r, fb_r, fd_s, fd_r, fa_s, fa_r, bx_r, bx_s, bc_r, bc_s,
):
    b = lax.axis_index("batch")
    f = lax.axis_index("feat")
    y, l = div(b, 2), rem(b, 2)
    z, h, c = div(f, 4), rem(div(f, 2), 2), rem(f, 2)
    xi = l * 4 + h * 2 + c

    def dev(y_, z_, h_, l_, c_):
        return (y_ * 2 + l_, z_ * 4 + h_ * 2 + c_)

    def ring_dev(y_, z_, xi_):
        return dev(y_, z_, rem(div(xi_, 2), 2), div(xi_, 4), rem(xi_, 2))

    def send(src, dst, s_sem, r_sem, to):
        pltpu.make_async_remote_copy(
            src_ref=src, dst_ref=dst, send_sem=s_sem, recv_sem=r_sem, device_id=to, device_id_type=MESH
        ).start()

    def wait(ref, sem):
        pltpu.make_async_copy(ref, ref, sem).wait()

    def loop(lo, hi, fn):
        def step(i, carry):
            fn(i)
            return carry

        lax.fori_loop(lo, hi, step, 0)

    def corr_to(q):
        return dev(2 * q + l, z, div(y, 4), h, rem(div(y, 2), 2))

    def corr_from(k, p):
        return dev(h * 4 + c * 2 + p, z, l, rem(y, 2), k)

    at_home = (rem(y, 2) == l) & (h == l) & (div(y, 2) == h * 2 + c)

    barrier = pltpu.get_barrier_semaphore()

    def greet(to):
        pl.semaphore_signal(barrier, inc=1, device_id=to, device_id_type=MESH)

    loop(1, 16, lambda e: greet((rem(b + e, 16), f)))
    loop(1, 8, lambda e: greet(ring_dev(y, z, rem(xi + e, 8))))
    loop(1, 8, lambda e: greet(dev(y, rem(z + e, 8), h, l, c)))
    loop(1, 8, lambda e: greet(dev(y, rem(z + e, 8), h, 1 - l, c)))
    for q in range(4):
        @pl.when(jnp.logical_not(at_home & (div(y, 2) == q)))
        def _(q=q):
            greet(corr_to(q))

        @pl.when(jnp.logical_not(at_home & (c == q // 2) & (rem(y, 2) == q % 2)))
        def _(q=q):
            greet(corr_from(q // 2, q % 2))

    wide_a = va[...].astype(f32)
    wide_b = vb[...].astype(f32)
    stat_own[0:1, :] = jnp.sum(wide_a, axis=0, keepdims=True)
    stat_own[1:2, :] = jnp.sum(wide_a * wide_a, axis=0, keepdims=True)
    stat_own[2:3, :] = jnp.sum(wide_b, axis=0, keepdims=True)
    stat_own[3:4, :] = jnp.sum(wide_b * wide_b, axis=0, keepdims=True)
    stat_own[4:8, :] = jnp.zeros((4, 128), f32)
    stats[b] = stat_own[...]

    pl.semaphore_wait(barrier, 15 + 7 + 7 + 7 + 8 - 2 * at_home.astype(jnp.int32))

    loop(1, 16, lambda e: send(stat_own, stats.at[b], st_s, st_r, (rem(b + e, 16), f)))

    half = rem(z, 2)
    native = half == l
    twin = xi + 1 - 2 * c

    def in_column(d):
        return dev(y, rem(z + d, 8), h, l, c)

    def slot_at(d):
        place = rem(z + d, 8)
        on = rem(rem(place, 2) + l + 1, 2)
        return (on * l + (1 - on) * (1 - l)) * 4 + div(rem(place + 7 + on, 8), 2)

    def spread_b():
        slot = slot_at(0)
        for i, d in enumerate((2, 6, 1, 7)):
            send(bbuf.at[slot], bbuf.at[slot], b_s.at[i], b_r.at[slot], in_column(d))

    def pass_b():
        for p, (frm, one, two) in enumerate(((6, 1, 2), (2, 7, 6))):
            slot = slot_at(frm)
            wait(bbuf.at[slot], b_r.at[slot])
            send(bbuf.at[slot], bbuf.at[slot], bp_s.at[p, 0], b_r.at[slot], in_column(one))
            part = bbuf.at[slot, pl.ds(p * 256, 256)]
            send(part, part, bp_s.at[p, 1], b_r.at[slot], in_column(two))

    @pl.when(native)
    def _():
        bbuf[slot_at(0)] = vb[...]
        spread_b()

    @pl.when(jnp.logical_not(native))
    def _():
        bown[...] = vb[...]
        slot = l * 4 + div(z, 2)
        send(bown, bbuf.at[slot], bx_s, bx_r, dev(y, rem(z + 1, 8), h, half, c))

    abuf[xi] = va[...]
    for i, e in enumerate((4, 2, 6)):
        send(abuf.at[xi], abuf.at[xi], a_s.at[i], a_r.at[xi], ring_dev(y, z, rem(xi + e, 8)))
    send(abuf.at[xi], abuf.at[xi], a_s.at[3], a_r.at[xi], ring_dev(y, z, twin))

    wait(stats.at[pl.ds(0, 15)], st_r)
    total = stats[0]
    for i in range(1, 16):
        total = total + stats[i]
    total = total / pairs
    mean_a, mean_b = total[0:1, :], total[2:3, :]
    inv_a = lax.rsqrt(total[1:2, :] - mean_a * mean_a + epsilon)
    inv_b = lax.rsqrt(total[3:4, :] - mean_b * mean_b + epsilon)
    own_ab = h * 2 + c
    astat[own_ab] = jnp.concatenate([mean_a, inv_a, mean_b, inv_b, jnp.zeros((4, 128), f32)], axis=0)
    for e in range(1, 4):
        to = rem(own_ab + e, 4)
        send(astat.at[own_ab], astat.at[own_ab], ms_s, as_r.at[own_ab], ring_dev(y, z, l * 4 + to))

    @pl.when(native)
    def _():
        own_q = div(z, 2)
        bstat[own_q] = astat[own_ab]
        for d in (1, 7, 2, 6, 3, 5, 4):
            send(bstat.at[own_q], bstat.at[own_q], ms_s, bs_r.at[own_q], in_column(d))

    @pl.when(native)
    def _():
        pass_b()

    @pl.when(jnp.logical_not(native))
    def _():
        wait(bbuf.at[slot_at(0)], bx_r)
        spread_b()

    for i, e in enumerate((4, 2, 6)):
        slot = rem(xi + e, 8)
        wait(abuf.at[slot], a_r.at[slot])
        send(abuf.at[slot], abuf.at[slot], a_s.at[4 + i], a_r.at[slot], ring_dev(y, z, twin))

    for e in range(1, 4):
        wait(astat.at[rem(own_ab + e, 4)], as_r.at[rem(own_ab + e, 4)])

    def turn(slot):
        which = rem(slot, 4)
        mean, inv = astat[which, 0:1, :], astat[which, 1:2, :]
        normed = ((abuf[slot].astype(f32) - mean) * inv).astype(bf16)
        anorm[slot] = normed
        aturn[which, :, pl.ds(pl.multiple_of(div(slot, 4) * 512, 512), 512)] = normed.T

    for e in (0, 4, 2, 6):
        turn(rem(xi + e, 8))

    @pl.when(jnp.logical_not(native))
    def _():
        pass_b()

    for e in (0, 4, 2, 6):
        slot = rem(twin + e, 8)
        wait(abuf.at[slot], a_r.at[slot])
        turn(slot)

    def side(buf, k):
        return jnp.concatenate([buf[k * 4 + i] for i in range(4)], axis=1)

    over_cols = (((1,), (1,)), ((), ()))
    over_in = (((1,), (0,)), ((), ()))

    def block(t):
        ahead = jnp.where(native, (0, 2, 4, 6)[t], (7, 5, 3, 1)[t])
        return div(rem(z + ahead, 8), 2)

    def along_y(e):
        return dev(rem(y + e, 8), z, h, l, c)

    def rows_of(to):
        return pl.ds(pl.multiple_of(to * 64, 64), 64)

    def correlate(t):
        q = block(t)
        late = 1 - half
        wait(bbuf.at[late * 4 + q], b_r.at[late * 4 + q])
        if t == 2:
            wait(bbuf.at[half * 4 + q], b_r.at[half * 4 + q])

        @pl.when(jnp.logical_not(native) | (div(z, 2) != q))
        def _():
            wait(bstat.at[q], bs_r.at[q])

        mean, inv = bstat[q, 2:3, :], bstat[q, 3:4, :]
        right = jnp.concatenate([bbuf[q], bbuf[4 + q]], axis=0)
        right = ((right.astype(f32) - mean) * inv).astype(bf16)
        bnorm[q] = right[:512]
        bnorm[4 + q] = right[512:]
        left = jnp.concatenate([aturn[i] for i in range(4)], axis=0)
        part = lax.dot_general(left, right, over_in, preferred_element_type=f32)
        cwide[t] = part
        cnarrow[t] = part.astype(bf16)

        def go(e, to, slot, sem, lo=0, n=64):
            piece = cnarrow.at[t, pl.ds(pl.multiple_of(rem(y + e, 8) * 64 + lo, 32), n)]
            send(piece, crecv.at[t, slot, pl.ds(lo, n)], c_s.at[t], sem, along_y(to))

        go(3, 1, 2, cp_r.at[t])
        go(5, 7, 3, cp_r.at[t])
        go(4, 6, 4, cp_r.at[t], 0, 32)
        go(4, 2, 5, cp_r.at[t], 32, 32)
        go(1, 1, 0, c_r.at[t])
        go(7, 7, 1, c_r.at[t])

    def pass_partial(t):
        wait(crecv.at[t, pl.ds(0, 3)], cp_r.at[t])
        up = cwide[t, rows_of(rem(y + 2, 8)), :] + crecv[t, 2].astype(f32)
        cpass[t, 0, 0:32, :] = up[:32].astype(bf16)
        cpass[t, 0, 32:64, :] = (up[32:] + crecv[t, 5, 32:64, :].astype(f32)).astype(bf16)
        send(cpass.at[t, 0], crecv.at[t, 6], cp_s.at[t], c_r.at[t], along_y(2))
        down = cwide[t, rows_of(rem(y + 6, 8)), :] + crecv[t, 3].astype(f32)
        cpass[t, 1, 0:32, :] = (down[:32] + crecv[t, 4, 0:32, :].astype(f32)).astype(bf16)
        cpass[t, 1, 32:64, :] = down[32:].astype(bf16)
        send(cpass.at[t, 1], crecv.at[t, 7], cp_s.at[t], c_r.at[t], along_y(6))

    def differentiate(t):
        q = block(t)
        wait(crecv.at[t, pl.ds(0, 4)], c_r.at[t])
        corr = cwide[t, rows_of(y), :]
        for i in (0, 1, 6, 7):
            corr = corr + crecv[t, i].astype(f32)
        corr = corr / pairs
        ctile[q] = corr
        row_ids = lax.broadcasted_iota(jnp.int32, corr.shape, 0)
        col_ids = lax.broadcasted_iota(jnp.int32, corr.shape, 1)
        here = jnp.where((z == 2 * q + l) & (div(y, 2) == h * 2 + c), rem(y, 2) * 64, 100000)
        grad = jnp.where(row_ids + here == col_ids, -2.0 * (1.0 - corr), 2.0 * off_weight * corr).astype(bf16)
        both = grad.astype(f32) * corr
        cols = jnp.sum(both, axis=0, keepdims=True)
        rows = jnp.sum(both.T, axis=0, keepdims=True)
        none = jnp.zeros_like(rows)
        rows = jnp.where(
            rem(y, 2) == 0, jnp.concatenate([rows, none], axis=1), jnp.concatenate([none, rows], axis=1)
        )
        terms = []
        for value in (cols, rows):
            high = value.astype(bf16).astype(f32)
            terms += [high, value - high]
        terms.append(jnp.zeros((12, 128), f32))
        gbuf[q, y, 0:64, :] = grad
        gbuf[q, y, 64:80, :] = jnp.concatenate(terms, axis=0).astype(bf16)
        send(gbuf.at[q, y], gbuf.at[q, y], g_s.at[t], gp_r.at[t], along_y(2))
        send(gbuf.at[q, y], gbuf.at[q, y], g_s.at[t], gp_r.at[t], along_y(6))
        send(gbuf.at[q, y], gbuf.at[q, y], g_s.at[t], g_r.at[t], along_y(1))
        send(gbuf.at[q, y], gbuf.at[q, y], g_s.at[t], g_r.at[t], along_y(7))

    def pass_gradient(t):
        q = block(t)
        wait(gbuf.at[q, pl.ds(0, 2)], gp_r.at[t])
        for frm, one, two, lo, n in ((6, 1, 2, 0, 48), (2, 7, 6, 48, 32)):
            item = gbuf.at[q, rem(y + frm, 8)]
            send(item, item, g_s.at[t], g_r.at[t], along_y(one))
            part = gbuf.at[q, rem(y + frm, 8), pl.ds(lo, n)]
            send(part, part, g_s.at[t], g_r.at[t], along_y(two))

    proj_a = [jnp.zeros((1, 128), f32)] * 4
    proj_b = []

    def take_gradient(t):
        q = block(t)
        wait(gbuf.at[q, pl.ds(0, 5)], g_r.at[t])
        total = jnp.zeros((1, 128), f32)
        for i in range(8):
            gfull[q, i * 64 : (i + 1) * 64, :] = gbuf[q, i, 0:64, :]
            sums = gbuf[q, i, 64:80, :].astype(f32)
            total = total + (sums[0:1, :] + sums[1:2, :])
            proj_a[i // 2] = proj_a[i // 2] + (sums[2:3, :] + sums[3:4, :])
        proj_b.append(total)

    def back_columns(t):
        q = block(t)
        for j in range(2):
            k = l if j == 0 else 1 - l
            left = jnp.concatenate([anorm[k * 4 + i] for i in range(4)], axis=1)
            back = lax.dot_general(left, gfull[q], over_in, preferred_element_type=f32)
            back = back - bnorm[k * 4 + q].astype(f32) * proj_b[t]
            if t != 2:
                bkeep[min(t, 2), j] = back
            bsend[t, j] = back.astype(bf16)

            def act(off):
                src = bsend.at[t, j]
                sem = fb_s.at[t, j]
                if off in (1, 7):
                    i = 0 if off == 1 else 1
                    send(src, bback.at[i], sem, fb_r.at[i], in_column(off))
                if off in (3, 5):
                    p = 0 if off == 3 else 1
                    send(src, bfull.at[p], sem, ff_r.at[p], in_column((1, 7)[p]))
                if off == 4:
                    for p, d in enumerate((2, 6)):
                        rows = pl.ds(256 - p * 256, 256)
                        send(bsend.at[t, j, rows], bhalf.at[p, rows], sem, fh_r.at[p], in_column(d))

            @pl.when(native)
            def _():
                act(offs_on[t][j])

            @pl.when(jnp.logical_not(native))
            def _():
                act(offs_off[t][j])

    def pass_back(p):
        d = (2, 6)[p]
        keep = bkeep.at[jnp.where(native, (1, 2)[p], (2, 1)[p]), jnp.where(native, 0, 1)]
        rows = pl.ds(256 - p * 256, 256)
        wait(bfull.at[p], ff_r.at[p])
        wait(bhalf.at[p, rows], fh_r.at[p])
        one = slice(256 - p * 256, 512 - p * 256)
        other = slice(p * 256, 256 + p * 256)
        bpass[p, other, :] = (keep[other, :] + bfull[p, other, :].astype(f32)).astype(bf16)
        bpass[p, one, :] = (keep[one, :] + bfull[p, one, :].astype(f32) + bhalf[p, one, :].astype(f32)).astype(bf16)
        send(bpass.at[p], bback.at[2 + p], fbp_s.at[p], fb_r.at[2 + p], in_column(d))

    correlate(0)
    correlate(1)
    pass_partial(0)
    correlate(2)
    pass_partial(1)
    differentiate(0)
    correlate(3)
    pass_partial(2)
    differentiate(1)
    pass_gradient(0)
    pass_partial(3)
    differentiate(2)
    pass_gradient(1)
    take_gradient(0)
    back_columns(0)
    differentiate(3)
    pass_gradient(2)
    take_gradient(1)
    back_columns(1)
    pass_gradient(3)
    take_gradient(2)
    back_columns(2)

    for q in range(4):
        stay = at_home & (div(y, 2) == q)

        @pl.when(stay)
        def _(q=q):
            corrb[c, rem(y, 2)] = ctile[q]

        @pl.when(jnp.logical_not(stay))
        def _(q=q):
            send(ctile.at[q], corrb.at[c, rem(y, 2)], o_s.at[q], o_r.at[c, rem(y, 2)], corr_to(q))

    take_gradient(3)
    whole_g = jnp.concatenate([gfull[q] for q in range(4)], axis=1)
    for k in range(2):
        back = lax.dot_general(side(bnorm, k), whole_g, over_cols, preferred_element_type=f32)
        for i in range(4):
            less = back[:, i * 128 : (i + 1) * 128] - anorm[k * 4 + i].astype(f32) * proj_a[i]
            akeep[k * 4 + i] = less
            asend[k * 4 + i] = less.astype(bf16)
    chip = l * 2 + h
    for e in (2, 1, 3, 0):
        to = rem(chip + e, 4)
        send(asend.at[to * 2 + 1 - c], ain.at[to], fd_s.at[e], fd_r.at[to], ring_dev(y, z, twin))

    @pl.when(native)
    def _():
        pass_back(0)

    @pl.when(jnp.logical_not(native))
    def _():
        pass_back(1)

    back_columns(3)

    @pl.when(native)
    def _():
        pass_back(1)

    @pl.when(jnp.logical_not(native))
    def _():
        pass_back(0)

    for e in (2, 1, 3, 0):
        to = rem(chip + e, 4)
        wait(ain.at[to], fd_r.at[to])
        summed = (akeep[to * 2 + c] + ain[to].astype(f32)).astype(bf16)
        if e:
            apass[e] = summed
            send(apass.at[e], aback.at[chip], fa_s.at[e], fa_r.at[chip], ring_dev(y, z, to * 2 + c))
        else:
            aback[chip] = summed

    for k in range(2):
        for p in range(2):
            @pl.when(jnp.logical_not(at_home & (c == k) & (rem(y, 2) == p)))
            def _(k=k, p=p):
                wait(corrb.at[k, p], o_r.at[k, p])

            co[p * 64 : (p + 1) * 64, k * 128 : (k + 1) * 128] = corrb[k, p]

    acc = bkeep[0, jnp.where(native, 0, 1)]
    for i in range(4):
        wait(bback.at[i], fb_r.at[i])
        acc = acc + bback[i].astype(f32)

    @pl.when(native)
    def _():
        gb[...] = (acc * inv_b).astype(bf16)

    @pl.when(jnp.logical_not(native))
    def _():
        wait(bown, bx_s)
        bown[...] = acc.astype(bf16)
        send(bown, bcross, bc_s, bc_r, dev(y, rem(z + 7, 8), h, 1 - l, c))

    for e in range(1, 4):
        frm = rem(chip + e, 4)
        wait(aback.at[frm], fa_r.at[frm])
    acc = aback[0].astype(f32)
    for i in range(1, 4):
        acc = acc + aback[i].astype(f32)
    ga[...] = (acc * inv_a).astype(bf16)

    @pl.when(jnp.logical_not(native))
    def _():
        wait(bcross, bc_r)
        gb[...] = (bcross[...].astype(f32) * inv_b).astype(bf16)

    @pl.when(native)
    def _():
        wait(stats.at[pl.ds(0, 10)], ms_s)

    @pl.when(jnp.logical_not(native))
    def _():
        wait(stats.at[pl.ds(0, 3)], ms_s)

    wait(stats.at[pl.ds(0, 15)], st_s)
    for i in range(7):
        wait(abuf.at[xi], a_s.at[i])
    for e in range(4):
        wait(asend.at[0], fd_s.at[e])
        if e:
            wait(apass.at[e], fa_s.at[e])

    @pl.when(jnp.logical_not(native))
    def _():
        wait(bown, bc_s)

    for i in range(4):
        wait(bbuf.at[0], b_s.at[i])
    for p in range(2):
        wait(bbuf.at[0], bp_s.at[p, 0])
        wait(bbuf.at[0, pl.ds(0, 256)], bp_s.at[p, 1])
        wait(bpass.at[p], fbp_s.at[p])

    for t in range(4):
        wait(crecv.at[t, pl.ds(0, 5)], c_s.at[t])
        wait(crecv.at[t, pl.ds(0, 2)], cp_s.at[t])
        wait(gbuf.at[t, pl.ds(0, 7)], g_s.at[t])

        @pl.when(jnp.logical_not(at_home & (div(y, 2) == t)))
        def _(t=t):
            wait(ctile.at[t], o_s.at[t])

        for j in range(2):
            goes_on = offs_on[t][j] not in (0, 2, 6)
            goes_off = offs_off[t][j] not in (0, 2, 6)
            if goes_on and goes_off:
                wait(bsend.at[t, j], fb_s.at[t, j])
            elif goes_on:
                @pl.when(native)
                def _(t=t, j=j):
                    wait(bsend.at[t, j], fb_s.at[t, j])
            elif goes_off:
                @pl.when(jnp.logical_not(native))
                def _(t=t, j=j):
                    wait(bsend.at[t, j], fb_s.at[t, j])


def body(view_a, view_b):
    rows, cols = view_a.shape
    pairs = rows * lax.axis_size("batch")
    vmem = pl.BlockSpec(memory_space=pltpu.VMEM)
    dma = pltpu.SemaphoreType.DMA

    def call(*args):
        return kernel(float(pairs), *args)

    return pl.pallas_call(
        call,
        name="barlow",
        out_shape=(
            jax.ShapeDtypeStruct((rows, cols), bf16),
            jax.ShapeDtypeStruct((rows, cols), bf16),
            jax.ShapeDtypeStruct((128, 256), f32),
        ),
        in_specs=[vmem, vmem],
        out_specs=(vmem, vmem, vmem),
        scratch_shapes=[
            pltpu.VMEM((8, 128), f32),
            pltpu.VMEM((16, 8, 128), f32),
            pltpu.VMEM((4, 8, 128), f32),
            pltpu.VMEM((4, 8, 128), f32),
            pltpu.VMEM((8, rows, 128), bf16),
            pltpu.VMEM((8, rows, 128), bf16),
            pltpu.VMEM((8, rows, 128), bf16),
            pltpu.VMEM((8, rows, 128), bf16),
            pltpu.VMEM((4, 128, 1024), bf16),
            pltpu.VMEM((4, 512, 128), f32),
            pltpu.VMEM((4, 512, 128), bf16),
            pltpu.VMEM((4, 8, 64, 128), bf16),
            pltpu.VMEM((4, 2, 64, 128), bf16),
            pltpu.VMEM((4, 64, 128), f32),
            pltpu.VMEM((2, 2, 64, 128), f32),
            pltpu.VMEM((4, 8, 80, 128), bf16),
            pltpu.VMEM((4, 512, 128), bf16),
            pltpu.VMEM((4, 2, rows, 128), bf16),
            pltpu.VMEM((3, 2, rows, 128), f32),
            pltpu.VMEM((2, rows, 128), bf16),
            pltpu.VMEM((2, rows, 128), bf16),
            pltpu.VMEM((2, rows, 128), bf16),
            pltpu.VMEM((4, rows, 128), bf16),
            pltpu.VMEM((rows, 128), bf16),
            pltpu.VMEM((rows, 128), bf16),
            pltpu.VMEM((8, rows, 128), bf16),
            pltpu.VMEM((8, rows, 128), f32),
            pltpu.VMEM((4, rows, 128), bf16),
            pltpu.VMEM((4, rows, 128), bf16),
            pltpu.VMEM((4, rows, 128), bf16),
            dma, dma, dma, dma((4,)), dma((4,)),
            dma((7,)), dma((8,)), dma((4,)), dma((8,)), dma((2, 2)),
            dma((4,)), dma((4,)), dma((4,)), dma((4,)), dma((4,)), dma((2, 2)), dma((4,)), dma((4,)), dma((4,)),
            dma((4, 2)), dma((2,)), dma((2,)), dma((2,)), dma((4,)),
            dma((4,)), dma((4,)), dma((4,)), dma((4,)), dma, dma, dma, dma,
        ],
        compiler_params=pltpu.CompilerParams(
            collective_id=0, has_side_effects=True, vmem_limit_bytes=40 * 2**20
        ),
    )(view_a, view_b)


def solution(mesh):
    return jax.shard_map(
        body,
        mesh=mesh,
        in_specs=(P("batch", "feat"), P("batch", "feat")),
        out_specs=(P("batch", "feat"), P("batch", "feat"), P("feat", "batch")),
        check_vma=False,
    )
```

```python
import jax
import jax.numpy as jnp
from jax import lax
from jax.experimental import pallas as pl
from jax.experimental.pallas import tpu as pltpu
from jax.sharding import PartitionSpec as P

MESH = pl.DeviceIdType.MESH
epsilon = 1e-05
off_weight = 0.0051
f32 = jnp.float32
bf16 = jnp.bfloat16


def div(a, n):
    return lax.div(a, jnp.int32(n))


def rem(a, n):
    return lax.rem(a, jnp.int32(n))


straight_c = ()
straight_g = ()

offs_on = ((0, 1), (2, 3), (4, 5), (6, 7))
offs_off = ((7, 0), (5, 6), (3, 4), (1, 2))


def kernel(
    pairs,
    view_a, view_b,
    ga, gb, co,
    va, vb, in_s,
    stat_own, stats, astat, bstat, abuf, bbuf, anorm, bnorm, aturn, cwide, cnarrow, crecv, cpass, ctile, corrb,
    gbuf, gfull, bsend, bkeep, bfull, bhalf, bpass, bback, bown, bcross, asend, akeep, ain, apass, aback,
    st_s, st_r, ms_s, as_r, bs_r, a_s, a_r, b_s, b_r, bp_s, c_s, cp_s, cp_r, c_r, o_s, o_r, g_s, gp_r, g_r,
    fb_s, fbp_s, ff_r, fh_r, fb_r, fd_s, fd_r, fa_s, fa_r, bx_r, bx_s, bc_r, bc_s,
):
    b = lax.axis_index("batch")
    f = lax.axis_index("feat")
    y, l = div(b, 2), rem(b, 2)
    z, h, c = div(f, 4), rem(div(f, 2), 2), rem(f, 2)
    xi = l * 4 + h * 2 + c

    def dev(y_, z_, h_, l_, c_):
        return (y_ * 2 + l_, z_ * 4 + h_ * 2 + c_)

    def ring_dev(y_, z_, xi_):
        return dev(y_, z_, rem(div(xi_, 2), 2), div(xi_, 4), rem(xi_, 2))

    def send(src, dst, s_sem, r_sem, to):
        pltpu.make_async_remote_copy(
            src_ref=src, dst_ref=dst, send_sem=s_sem, recv_sem=r_sem, device_id=to, device_id_type=MESH
        ).start()

    def wait(ref, sem):
        pltpu.make_async_copy(ref, ref, sem).wait()

    def loop(lo, hi, fn):
        def step(i, carry):
            fn(i)
            return carry

        lax.fori_loop(lo, hi, step, 0)

    def corr_to(q):
        return dev(2 * q + l, z, div(y, 4), h, rem(div(y, 2), 2))

    def corr_from(k, p):
        return dev(h * 4 + c * 2 + p, z, l, rem(y, 2), k)

    at_home = (rem(y, 2) == l) & (h == l) & (div(y, 2) == h * 2 + c)

    pltpu.make_async_copy(view_a, va, in_s.at[0]).start()
    pltpu.make_async_copy(view_b, vb, in_s.at[1]).start()

    barrier = pltpu.get_barrier_semaphore()

    def greet(to):
        pl.semaphore_signal(barrier, inc=1, device_id=to, device_id_type=MESH)

    loop(1, 16, lambda e: greet((rem(b + e, 16), f)))
    loop(1, 8, lambda e: greet(ring_dev(y, z, rem(xi + e, 8))))
    loop(1, 8, lambda e: greet(dev(y, rem(z + e, 8), h, l, c)))
    loop(1, 8, lambda e: greet(dev(y, rem(z + e, 8), h, 1 - l, c)))
    for q in range(4):
        @pl.when(jnp.logical_not(at_home & (div(y, 2) == q)))
        def _(q=q):
            greet(corr_to(q))

        @pl.when(jnp.logical_not(at_home & (c == q // 2) & (rem(y, 2) == q % 2)))
        def _(q=q):
            greet(corr_from(q // 2, q % 2))

    wait(va, in_s.at[0])
    wait(vb, in_s.at[1])
    wide_a = va[...].astype(f32)
    wide_b = vb[...].astype(f32)
    stat_own[0:1, :] = jnp.sum(wide_a, axis=0, keepdims=True)
    stat_own[1:2, :] = jnp.sum(wide_a * wide_a, axis=0, keepdims=True)
    stat_own[2:3, :] = jnp.sum(wide_b, axis=0, keepdims=True)
    stat_own[3:4, :] = jnp.sum(wide_b * wide_b, axis=0, keepdims=True)
    stat_own[4:8, :] = jnp.zeros((4, 128), f32)
    stats[b] = stat_own[...]

    pl.semaphore_wait(barrier, 15 + 7 + 7 + 7 + 8 - 2 * at_home.astype(jnp.int32))

    loop(1, 16, lambda e: send(stat_own, stats.at[b], st_s, st_r, (rem(b + e, 16), f)))

    half = rem(z, 2)
    native = half == l
    twin = xi + 1 - 2 * c

    def in_column(d):
        return dev(y, rem(z + d, 8), h, l, c)

    def slot_at(d):
        place = rem(z + d, 8)
        on = rem(rem(place, 2) + l + 1, 2)
        return (on * l + (1 - on) * (1 - l)) * 4 + div(rem(place + 7 + on, 8), 2)

    def spread_b():
        slot = slot_at(0)
        for i, d in enumerate((2, 6, 1, 7)):
            send(bbuf.at[slot], bbuf.at[slot], b_s.at[i], b_r.at[slot], in_column(d))

    def pass_b():
        for p, (frm, one, two) in enumerate(((6, 1, 2), (2, 7, 6))):
            slot = slot_at(frm)
            wait(bbuf.at[slot], b_r.at[slot])
            send(bbuf.at[slot], bbuf.at[slot], bp_s.at[p, 0], b_r.at[slot], in_column(one))
            part = bbuf.at[slot, pl.ds(p * 256, 256)]
            send(part, part, bp_s.at[p, 1], b_r.at[slot], in_column(two))

    @pl.when(native)
    def _():
        bbuf[slot_at(0)] = vb[...]
        spread_b()

    @pl.when(jnp.logical_not(native))
    def _():
        bown[...] = vb[...]
        slot = l * 4 + div(z, 2)
        send(bown, bbuf.at[slot], bx_s, bx_r, dev(y, rem(z + 1, 8), h, half, c))

    abuf[xi] = va[...]
    for i, e in enumerate((4, 2, 6)):
        send(abuf.at[xi], abuf.at[xi], a_s.at[i], a_r.at[xi], ring_dev(y, z, rem(xi + e, 8)))
    send(abuf.at[xi], abuf.at[xi], a_s.at[3], a_r.at[xi], ring_dev(y, z, twin))

    wait(stats.at[pl.ds(0, 15)], st_r)
    total = stats[0]
    for i in range(1, 16):
        total = total + stats[i]
    total = total / pairs
    mean_a, mean_b = total[0:1, :], total[2:3, :]
    inv_a = lax.rsqrt(total[1:2, :] - mean_a * mean_a + epsilon)
    inv_b = lax.rsqrt(total[3:4, :] - mean_b * mean_b + epsilon)
    own_ab = h * 2 + c
    astat[own_ab] = jnp.concatenate([mean_a, inv_a, mean_b, inv_b, jnp.zeros((4, 128), f32)], axis=0)
    for e in range(1, 4):
        to = rem(own_ab + e, 4)
        send(astat.at[own_ab], astat.at[own_ab], ms_s, as_r.at[own_ab], ring_dev(y, z, l * 4 + to))

    @pl.when(native)
    def _():
        own_q = div(z, 2)
        bstat[own_q] = astat[own_ab]
        for d in (1, 7, 2, 6, 3, 5, 4):
            send(bstat.at[own_q], bstat.at[own_q], ms_s, bs_r.at[own_q], in_column(d))

    @pl.when(native)
    def _():
        pass_b()

    @pl.when(jnp.logical_not(native))
    def _():
        wait(bbuf.at[slot_at(0)], bx_r)
        spread_b()

    for i, e in enumerate((4, 2, 6)):
        slot = rem(xi + e, 8)
        wait(abuf.at[slot], a_r.at[slot])
        send(abuf.at[slot], abuf.at[slot], a_s.at[4 + i], a_r.at[slot], ring_dev(y, z, twin))

    for e in range(1, 4):
        wait(astat.at[rem(own_ab + e, 4)], as_r.at[rem(own_ab + e, 4)])

    def turn(slot):
        which = rem(slot, 4)
        mean, inv = astat[which, 0:1, :], astat[which, 1:2, :]
        normed = ((abuf[slot].astype(f32) - mean) * inv).astype(bf16)
        anorm[slot] = normed
        aturn[which, :, pl.ds(pl.multiple_of(div(slot, 4) * 512, 512), 512)] = normed.T

    for e in (0, 4, 2, 6):
        turn(rem(xi + e, 8))

    @pl.when(jnp.logical_not(native))
    def _():
        pass_b()

    for e in (0, 4, 2, 6):
        slot = rem(twin + e, 8)
        wait(abuf.at[slot], a_r.at[slot])
        turn(slot)

    def side(buf, k):
        return jnp.concatenate([buf[k * 4 + i] for i in range(4)], axis=1)

    over_cols = (((1,), (1,)), ((), ()))
    over_in = (((1,), (0,)), ((), ()))

    def block(t):
        ahead = jnp.where(native, (0, 2, 4, 6)[t], (7, 5, 3, 1)[t])
        return div(rem(z + ahead, 8), 2)

    def along_y(e):
        return dev(rem(y + e, 8), z, h, l, c)

    def rows_of(to):
        return pl.ds(pl.multiple_of(to * 64, 64), 64)

    def correlate(t):
        q = block(t)
        late = 1 - half
        wait(bbuf.at[late * 4 + q], b_r.at[late * 4 + q])
        if t == 2:
            wait(bbuf.at[half * 4 + q], b_r.at[half * 4 + q])

        @pl.when(jnp.logical_not(native) | (div(z, 2) != q))
        def _():
            wait(bstat.at[q], bs_r.at[q])

        mean, inv = bstat[q, 2:3, :], bstat[q, 3:4, :]
        right = jnp.concatenate([bbuf[q], bbuf[4 + q]], axis=0)
        right = ((right.astype(f32) - mean) * inv).astype(bf16)
        bnorm[q] = right[:512]
        bnorm[4 + q] = right[512:]
        left = jnp.concatenate([aturn[i] for i in range(4)], axis=0)
        part = lax.dot_general(left, right, over_in, preferred_element_type=f32)
        cwide[t] = part
        cnarrow[t] = part.astype(bf16)

        def go(e, to, slot, sem, lo=0, n=64):
            piece = cnarrow.at[t, pl.ds(pl.multiple_of(rem(y + e, 8) * 64 + lo, 32), n)]
            send(piece, crecv.at[t, slot, pl.ds(lo, n)], c_s.at[t], sem, along_y(to))

        if t in straight_c:
            for e in (4, 3, 5, 2, 6, 1, 7):
                go(e, e, e, c_r.at[t])
            return
        go(3, 1, 2, cp_r.at[t])
        go(5, 7, 3, cp_r.at[t])
        go(4, 6, 4, cp_r.at[t], 0, 32)
        go(4, 2, 5, cp_r.at[t], 32, 32)
        go(1, 1, 0, c_r.at[t])
        go(7, 7, 1, c_r.at[t])

    def pass_partial(t):
        if t in straight_c:
            return
        wait(crecv.at[t, pl.ds(0, 3)], cp_r.at[t])
        up = cwide[t, rows_of(rem(y + 2, 8)), :] + crecv[t, 2].astype(f32)
        cpass[t, 0, 0:32, :] = up[:32].astype(bf16)
        cpass[t, 0, 32:64, :] = (up[32:] + crecv[t, 5, 32:64, :].astype(f32)).astype(bf16)
        send(cpass.at[t, 0], crecv.at[t, 6], cp_s.at[t], c_r.at[t], along_y(2))
        down = cwide[t, rows_of(rem(y + 6, 8)), :] + crecv[t, 3].astype(f32)
        cpass[t, 1, 0:32, :] = (down[:32] + crecv[t, 4, 0:32, :].astype(f32)).astype(bf16)
        cpass[t, 1, 32:64, :] = down[32:].astype(bf16)
        send(cpass.at[t, 1], crecv.at[t, 7], cp_s.at[t], c_r.at[t], along_y(6))

    def differentiate(t):
        q = block(t)
        straight = t in straight_c
        wait(crecv.at[t, pl.ds(0, 7 if straight else 4)], c_r.at[t])
        corr = cwide[t, rows_of(y), :]
        for i in range(1, 8) if straight else (0, 1, 6, 7):
            corr = corr + crecv[t, i].astype(f32)
        corr = corr / pairs
        ctile[q] = corr
        row_ids = lax.broadcasted_iota(jnp.int32, corr.shape, 0)
        col_ids = lax.broadcasted_iota(jnp.int32, corr.shape, 1)
        here = jnp.where((z == 2 * q + l) & (div(y, 2) == h * 2 + c), rem(y, 2) * 64, 100000)
        grad = jnp.where(row_ids + here == col_ids, -2.0 * (1.0 - corr), 2.0 * off_weight * corr).astype(bf16)
        both = grad.astype(f32) * corr
        cols = jnp.sum(both, axis=0, keepdims=True)
        rows = jnp.sum(both.T, axis=0, keepdims=True)
        none = jnp.zeros_like(rows)
        rows = jnp.where(
            rem(y, 2) == 0, jnp.concatenate([rows, none], axis=1), jnp.concatenate([none, rows], axis=1)
        )
        terms = []
        for value in (cols, rows):
            high = value.astype(bf16).astype(f32)
            terms += [high, value - high]
        terms.append(jnp.zeros((12, 128), f32))
        gbuf[q, y, 0:64, :] = grad
        gbuf[q, y, 64:80, :] = jnp.concatenate(terms, axis=0).astype(bf16)
        if t in straight_g:
            for e in (4, 3, 5, 2, 6, 1, 7):
                send(gbuf.at[q, y], gbuf.at[q, y], g_s.at[t], g_r.at[t], along_y(e))
            return
        send(gbuf.at[q, y], gbuf.at[q, y], g_s.at[t], gp_r.at[t], along_y(2))
        send(gbuf.at[q, y], gbuf.at[q, y], g_s.at[t], gp_r.at[t], along_y(6))
        send(gbuf.at[q, y], gbuf.at[q, y], g_s.at[t], g_r.at[t], along_y(1))
        send(gbuf.at[q, y], gbuf.at[q, y], g_s.at[t], g_r.at[t], along_y(7))

    def pass_gradient(t):
        if t in straight_g:
            return
        q = block(t)
        wait(gbuf.at[q, pl.ds(0, 2)], gp_r.at[t])
        for frm, one, two, lo, n in ((6, 1, 2, 0, 48), (2, 7, 6, 48, 32)):
            item = gbuf.at[q, rem(y + frm, 8)]
            send(item, item, g_s.at[t], g_r.at[t], along_y(one))
            part = gbuf.at[q, rem(y + frm, 8), pl.ds(lo, n)]
            send(part, part, g_s.at[t], g_r.at[t], along_y(two))

    proj_a = [jnp.zeros((1, 128), f32)] * 4
    proj_b = []

    def take_gradient(t):
        q = block(t)
        wait(gbuf.at[q, pl.ds(0, 7 if t in straight_g else 5)], g_r.at[t])
        total = jnp.zeros((1, 128), f32)
        for i in range(8):
            gfull[q, i * 64 : (i + 1) * 64, :] = gbuf[q, i, 0:64, :]
            sums = gbuf[q, i, 64:80, :].astype(f32)
            total = total + (sums[0:1, :] + sums[1:2, :])
            proj_a[i // 2] = proj_a[i // 2] + (sums[2:3, :] + sums[3:4, :])
        proj_b.append(total)

    def back_columns(t):
        q = block(t)
        for j in range(2):
            k = l if j == 0 else 1 - l
            left = jnp.concatenate([anorm[k * 4 + i] for i in range(4)], axis=1)
            back = lax.dot_general(left, gfull[q], over_in, preferred_element_type=f32)
            back = back - bnorm[k * 4 + q].astype(f32) * proj_b[t]
            if t != 2:
                bkeep[min(t, 2), j] = back
            bsend[t, j] = back.astype(bf16)

            def act(off):
                src = bsend.at[t, j]
                sem = fb_s.at[t, j]
                if off in (1, 7):
                    i = 0 if off == 1 else 1
                    send(src, bback.at[i], sem, fb_r.at[i], in_column(off))
                if off in (3, 5):
                    p = 0 if off == 3 else 1
                    send(src, bfull.at[p], sem, ff_r.at[p], in_column((1, 7)[p]))
                if off == 4:
                    for p, d in enumerate((2, 6)):
                        rows = pl.ds(256 - p * 256, 256)
                        send(bsend.at[t, j, rows], bhalf.at[p, rows], sem, fh_r.at[p], in_column(d))

            @pl.when(native)
            def _():
                act(offs_on[t][j])

            @pl.when(jnp.logical_not(native))
            def _():
                act(offs_off[t][j])

    def pass_back(p):
        d = (2, 6)[p]
        keep = bkeep.at[jnp.where(native, (1, 2)[p], (2, 1)[p]), jnp.where(native, 0, 1)]
        rows = pl.ds(256 - p * 256, 256)
        wait(bfull.at[p], ff_r.at[p])
        wait(bhalf.at[p, rows], fh_r.at[p])
        one = slice(256 - p * 256, 512 - p * 256)
        other = slice(p * 256, 256 + p * 256)
        bpass[p, other, :] = (keep[other, :] + bfull[p, other, :].astype(f32)).astype(bf16)
        bpass[p, one, :] = (keep[one, :] + bfull[p, one, :].astype(f32) + bhalf[p, one, :].astype(f32)).astype(bf16)
        send(bpass.at[p], bback.at[2 + p], fbp_s.at[p], fb_r.at[2 + p], in_column(d))

    correlate(0)
    correlate(1)
    pass_partial(0)
    correlate(2)
    pass_partial(1)
    differentiate(0)
    correlate(3)
    pass_partial(2)
    differentiate(1)
    pass_gradient(0)
    pass_partial(3)
    differentiate(2)
    pass_gradient(1)
    take_gradient(0)
    back_columns(0)
    differentiate(3)
    pass_gradient(2)
    take_gradient(1)
    back_columns(1)
    pass_gradient(3)
    take_gradient(2)
    back_columns(2)

    for q in range(4):
        stay = at_home & (div(y, 2) == q)

        @pl.when(stay)
        def _(q=q):
            corrb[c, rem(y, 2)] = ctile[q]

        @pl.when(jnp.logical_not(stay))
        def _(q=q):
            send(ctile.at[q], corrb.at[c, rem(y, 2)], o_s.at[q], o_r.at[c, rem(y, 2)], corr_to(q))

    take_gradient(3)
    whole_g = jnp.concatenate([gfull[q] for q in range(4)], axis=1)
    for k in range(2):
        back = lax.dot_general(side(bnorm, k), whole_g, over_cols, preferred_element_type=f32)
        for i in range(4):
            less = back[:, i * 128 : (i + 1) * 128] - anorm[k * 4 + i].astype(f32) * proj_a[i]
            akeep[k * 4 + i] = less
            asend[k * 4 + i] = less.astype(bf16)
    chip = l * 2 + h
    for e in (2, 1, 3, 0):
        to = rem(chip + e, 4)
        send(asend.at[to * 2 + 1 - c], ain.at[to], fd_s.at[e], fd_r.at[to], ring_dev(y, z, twin))

    @pl.when(native)
    def _():
        pass_back(0)

    @pl.when(jnp.logical_not(native))
    def _():
        pass_back(1)

    back_columns(3)

    @pl.when(native)
    def _():
        pass_back(1)

    @pl.when(jnp.logical_not(native))
    def _():
        pass_back(0)

    for e in (2, 1, 3, 0):
        to = rem(chip + e, 4)
        wait(ain.at[to], fd_r.at[to])
        summed = (akeep[to * 2 + c] + ain[to].astype(f32)).astype(bf16)
        if e:
            apass[e] = summed
            send(apass.at[e], aback.at[chip], fa_s.at[e], fa_r.at[chip], ring_dev(y, z, to * 2 + c))
        else:
            aback[chip] = summed

    for k in range(2):
        for p in range(2):
            @pl.when(jnp.logical_not(at_home & (c == k) & (rem(y, 2) == p)))
            def _(k=k, p=p):
                wait(corrb.at[k, p], o_r.at[k, p])

            co[p * 64 : (p + 1) * 64, k * 128 : (k + 1) * 128] = corrb[k, p]

    acc = bkeep[0, jnp.where(native, 0, 1)]
    for i in range(4):
        wait(bback.at[i], fb_r.at[i])
        acc = acc + bback[i].astype(f32)

    @pl.when(native)
    def _():
        gb[...] = (acc * inv_b).astype(bf16)

    @pl.when(jnp.logical_not(native))
    def _():
        wait(bown, bx_s)
        bown[...] = acc.astype(bf16)
        send(bown, bcross, bc_s, bc_r, dev(y, rem(z + 7, 8), h, 1 - l, c))

    for e in range(1, 4):
        frm = rem(chip + e, 4)
        wait(aback.at[frm], fa_r.at[frm])
    acc = aback[0].astype(f32)
    for i in range(1, 4):
        acc = acc + aback[i].astype(f32)
    ga[...] = (acc * inv_a).astype(bf16)

    @pl.when(jnp.logical_not(native))
    def _():
        wait(bcross, bc_r)
        gb[...] = (bcross[...].astype(f32) * inv_b).astype(bf16)

    @pl.when(native)
    def _():
        wait(stats.at[pl.ds(0, 10)], ms_s)

    @pl.when(jnp.logical_not(native))
    def _():
        wait(stats.at[pl.ds(0, 3)], ms_s)

    wait(stats.at[pl.ds(0, 15)], st_s)
    for i in range(7):
        wait(abuf.at[xi], a_s.at[i])
    for e in range(4):
        wait(asend.at[0], fd_s.at[e])
        if e:
            wait(apass.at[e], fa_s.at[e])

    @pl.when(jnp.logical_not(native))
    def _():
        wait(bown, bc_s)

    for i in range(4):
        wait(bbuf.at[0], b_s.at[i])
    for p in range(2):
        wait(bbuf.at[0], bp_s.at[p, 0])
        wait(bbuf.at[0, pl.ds(0, 256)], bp_s.at[p, 1])
        wait(bpass.at[p], fbp_s.at[p])

    for t in range(4):
        wait(crecv.at[t, pl.ds(0, 7 if t in straight_c else 5)], c_s.at[t])
        if t not in straight_c:
            wait(crecv.at[t, pl.ds(0, 2)], cp_s.at[t])
        wait(gbuf.at[t, pl.ds(0, 7)], g_s.at[t])

        @pl.when(jnp.logical_not(at_home & (div(y, 2) == t)))
        def _(t=t):
            wait(ctile.at[t], o_s.at[t])

        for j in range(2):
            goes_on = offs_on[t][j] not in (0, 2, 6)
            goes_off = offs_off[t][j] not in (0, 2, 6)
            if goes_on and goes_off:
                wait(bsend.at[t, j], fb_s.at[t, j])
            elif goes_on:
                @pl.when(native)
                def _(t=t, j=j):
                    wait(bsend.at[t, j], fb_s.at[t, j])
            elif goes_off:
                @pl.when(jnp.logical_not(native))
                def _(t=t, j=j):
                    wait(bsend.at[t, j], fb_s.at[t, j])


def body(view_a, view_b):
    rows, cols = view_a.shape
    pairs = rows * lax.axis_size("batch")
    vmem = pl.BlockSpec(memory_space=pltpu.VMEM)
    dma = pltpu.SemaphoreType.DMA

    def call(*args):
        return kernel(float(pairs), *args)

    results = pl.pallas_call(
        call,
        name="barlow",
        out_shape=(
            jax.ShapeDtypeStruct((rows, cols), bf16),
            jax.ShapeDtypeStruct((rows, cols), bf16),
            jax.ShapeDtypeStruct((128, 256), f32),
        ),
        in_specs=[pl.BlockSpec(memory_space=pltpu.HBM)] * 2,
        out_specs=(vmem, vmem, vmem),
        scratch_shapes=[
            pltpu.VMEM((rows, cols), bf16),
            pltpu.VMEM((rows, cols), bf16),
            dma((2,)),
            pltpu.VMEM((8, 128), f32),
            pltpu.VMEM((16, 8, 128), f32),
            pltpu.VMEM((4, 8, 128), f32),
            pltpu.VMEM((4, 8, 128), f32),
            pltpu.VMEM((8, rows, 128), bf16),
            pltpu.VMEM((8, rows, 128), bf16),
            pltpu.VMEM((8, rows, 128), bf16),
            pltpu.VMEM((8, rows, 128), bf16),
            pltpu.VMEM((4, 128, 1024), bf16),
            pltpu.VMEM((4, 512, 128), f32),
            pltpu.VMEM((4, 512, 128), bf16),
            pltpu.VMEM((4, 8, 64, 128), bf16),
            pltpu.VMEM((4, 2, 64, 128), bf16),
            pltpu.VMEM((4, 64, 128), f32),
            pltpu.VMEM((2, 2, 64, 128), f32),
            pltpu.VMEM((4, 8, 80, 128), bf16),
            pltpu.VMEM((4, 512, 128), bf16),
            pltpu.VMEM((4, 2, rows, 128), bf16),
            pltpu.VMEM((3, 2, rows, 128), f32),
            pltpu.VMEM((2, rows, 128), bf16),
            pltpu.VMEM((2, rows, 128), bf16),
            pltpu.VMEM((2, rows, 128), bf16),
            pltpu.VMEM((4, rows, 128), bf16),
            pltpu.VMEM((rows, 128), bf16),
            pltpu.VMEM((rows, 128), bf16),
            pltpu.VMEM((8, rows, 128), bf16),
            pltpu.VMEM((8, rows, 128), f32),
            pltpu.VMEM((4, rows, 128), bf16),
            pltpu.VMEM((4, rows, 128), bf16),
            pltpu.VMEM((4, rows, 128), bf16),
            dma, dma, dma, dma((4,)), dma((4,)),
            dma((7,)), dma((8,)), dma((4,)), dma((8,)), dma((2, 2)),
            dma((4,)), dma((4,)), dma((4,)), dma((4,)), dma((4,)), dma((2, 2)), dma((4,)), dma((4,)), dma((4,)),
            dma((4, 2)), dma((2,)), dma((2,)), dma((2,)), dma((4,)),
            dma((4,)), dma((4,)), dma((4,)), dma((4,)), dma, dma, dma, dma,
        ],
        compiler_params=pltpu.CompilerParams(
            collective_id=0, has_side_effects=True, vmem_limit_bytes=60 * 2**20
        ),
    )(view_a, view_b)

    def place(grad_a, grad_b, corr, out_a, out_b, out_c, sems):
        copies = [
            pltpu.make_async_copy(src, dst, sems.at[i])
            for i, (src, dst) in enumerate(((grad_a, out_a), (grad_b, out_b), (corr, out_c)))
        ]
        for copy in copies:
            copy.start()
        for copy in copies:
            copy.wait()

    anywhere = pl.BlockSpec(memory_space=pl.ANY)
    return pl.pallas_call(
        place,
        name="place",
        out_shape=tuple(jax.ShapeDtypeStruct(r.shape, r.dtype) for r in results),
        in_specs=[vmem] * 3,
        out_specs=(anywhere,) * 3,
        scratch_shapes=[dma((3,))],
    )(*results)


def solution(mesh):
    return jax.shard_map(
        body,
        mesh=mesh,
        in_specs=(P("batch", "feat"), P("batch", "feat")),
        out_specs=(P("batch", "feat"), P("batch", "feat"), P("feat", "batch")),
        check_vma=False,
    )
```

```python
import jax
import jax.numpy as jnp
from jax import lax
from jax.experimental import pallas as pl
from jax.experimental.pallas import tpu as pltpu
from jax.sharding import PartitionSpec as P

MESH = pl.DeviceIdType.MESH
epsilon = 1e-05
off_weight = 0.0051
f32 = jnp.float32
bf16 = jnp.bfloat16


def div(a, n):
    return lax.div(a, jnp.int32(n))


def rem(a, n):
    return lax.rem(a, jnp.int32(n))


straight_c = ()
straight_g = ()

offs_on = ((0, 1), (2, 3), (4, 5), (6, 7))
offs_off = ((7, 0), (5, 6), (3, 4), (1, 2))


def kernel(
    pairs,
    view_a, view_b,
    ga, gb, co,
    va, vb, in_s,
    stat_own, stats, astat, bstat, abuf, bbuf, anorm, bnorm, aturn, cwide, cnarrow, crecv, cpass, ctile, corrb,
    gbuf, gfull, bsend, bkeep, bfull, bhalf, bpass, bback, bown, bcross, asend, akeep, ain, apass, aback,
    st_s, st_r, ms_s, as_r, bs_r, a_s, a_r, b_s, b_r, bp_s, c_s, cp_s, cp_r, c_r, o_s, o_r, g_s, gp_r, g_r,
    fb_s, fbp_s, ff_r, fh_r, fb_r, fd_s, fd_r, fa_s, fa_r, bx_r, bx_s, bc_r, bc_s,
):
    b = lax.axis_index("batch")
    f = lax.axis_index("feat")
    y, l = div(b, 2), rem(b, 2)
    z, h, c = div(f, 4), rem(div(f, 2), 2), rem(f, 2)
    xi = l * 4 + h * 2 + c

    def dev(y_, z_, h_, l_, c_):
        return (y_ * 2 + l_, z_ * 4 + h_ * 2 + c_)

    def ring_dev(y_, z_, xi_):
        return dev(y_, z_, rem(div(xi_, 2), 2), div(xi_, 4), rem(xi_, 2))

    def send(src, dst, s_sem, r_sem, to):
        pltpu.make_async_remote_copy(
            src_ref=src, dst_ref=dst, send_sem=s_sem, recv_sem=r_sem, device_id=to, device_id_type=MESH
        ).start()

    def wait(ref, sem):
        pltpu.make_async_copy(ref, ref, sem).wait()

    def loop(lo, hi, fn):
        def step(i, carry):
            fn(i)
            return carry

        lax.fori_loop(lo, hi, step, 0)

    def corr_to(q):
        return dev(2 * q + l, z, div(y, 4), h, rem(div(y, 2), 2))

    def corr_from(k, p):
        return dev(h * 4 + c * 2 + p, z, l, rem(y, 2), k)

    at_home = (rem(y, 2) == l) & (h == l) & (div(y, 2) == h * 2 + c)

    pltpu.make_async_copy(view_a, va, in_s.at[0]).start()
    pltpu.make_async_copy(view_b, vb, in_s.at[1]).start()

    barrier = pltpu.get_barrier_semaphore()

    def greet(to):
        pl.semaphore_signal(barrier, inc=1, device_id=to, device_id_type=MESH)

    loop(1, 16, lambda e: greet((rem(b + e, 16), f)))
    loop(1, 8, lambda e: greet(ring_dev(y, z, rem(xi + e, 8))))
    loop(1, 8, lambda e: greet(dev(y, rem(z + e, 8), h, l, c)))
    loop(1, 8, lambda e: greet(dev(y, rem(z + e, 8), h, 1 - l, c)))
    for q in range(4):
        @pl.when(jnp.logical_not(at_home & (div(y, 2) == q)))
        def _(q=q):
            greet(corr_to(q))

        @pl.when(jnp.logical_not(at_home & (c == q // 2) & (rem(y, 2) == q % 2)))
        def _(q=q):
            greet(corr_from(q // 2, q % 2))

    wait(va, in_s.at[0])
    wait(vb, in_s.at[1])
    wide_a = va[...].astype(f32)
    wide_b = vb[...].astype(f32)
    stat_own[0:1, :] = jnp.sum(wide_a, axis=0, keepdims=True)
    stat_own[1:2, :] = jnp.sum(wide_a * wide_a, axis=0, keepdims=True)
    stat_own[2:3, :] = jnp.sum(wide_b, axis=0, keepdims=True)
    stat_own[3:4, :] = jnp.sum(wide_b * wide_b, axis=0, keepdims=True)
    stat_own[4:8, :] = jnp.zeros((4, 128), f32)
    stats[b] = stat_own[...]

    pl.semaphore_wait(barrier, 15 + 7 + 7 + 7 + 8 - 2 * at_home.astype(jnp.int32))

    loop(1, 16, lambda e: send(stat_own, stats.at[b], st_s, st_r, (rem(b + e, 16), f)))

    half = rem(z, 2)
    native = half == l
    twin = xi + 1 - 2 * c

    def in_column(d):
        return dev(y, rem(z + d, 8), h, l, c)

    def slot_at(d):
        place = rem(z + d, 8)
        on = rem(rem(place, 2) + l + 1, 2)
        return (on * l + (1 - on) * (1 - l)) * 4 + div(rem(place + 7 + on, 8), 2)

    def spread_b():
        slot = slot_at(0)
        for i, d in enumerate((2, 6, 1, 7)):
            send(bbuf.at[slot], bbuf.at[slot], b_s.at[i], b_r.at[slot], in_column(d))

    def pass_b():
        for p, (frm, one, two) in enumerate(((6, 1, 2), (2, 7, 6))):
            slot = slot_at(frm)
            wait(bbuf.at[slot], b_r.at[slot])
            send(bbuf.at[slot], bbuf.at[slot], bp_s.at[p, 0], b_r.at[slot], in_column(one))
            part = bbuf.at[slot, pl.ds(p * 256, 256)]
            send(part, part, bp_s.at[p, 1], b_r.at[slot], in_column(two))

    @pl.when(native)
    def _():
        bbuf[slot_at(0)] = vb[...]
        spread_b()

    @pl.when(jnp.logical_not(native))
    def _():
        bown[...] = vb[...]
        slot = l * 4 + div(z, 2)
        send(bown, bbuf.at[slot], bx_s, bx_r, dev(y, rem(z + 1, 8), h, half, c))

    abuf[xi] = va[...]
    for i, e in enumerate((4, 2, 6)):
        send(abuf.at[xi], abuf.at[xi], a_s.at[i], a_r.at[xi], ring_dev(y, z, rem(xi + e, 8)))
    send(abuf.at[xi], abuf.at[xi], a_s.at[3], a_r.at[xi], ring_dev(y, z, twin))

    @pl.when(native)
    def _():
        pass_b()

    @pl.when(jnp.logical_not(native))
    def _():
        wait(bbuf.at[slot_at(0)], bx_r)
        spread_b()

    wait(stats.at[pl.ds(0, 15)], st_r)
    total = stats[0]
    for i in range(1, 16):
        total = total + stats[i]
    total = total / pairs
    mean_a, mean_b = total[0:1, :], total[2:3, :]
    inv_a = lax.rsqrt(total[1:2, :] - mean_a * mean_a + epsilon)
    inv_b = lax.rsqrt(total[3:4, :] - mean_b * mean_b + epsilon)
    own_ab = h * 2 + c
    astat[own_ab] = jnp.concatenate([mean_a, inv_a, mean_b, inv_b, jnp.zeros((4, 128), f32)], axis=0)
    for e in range(1, 4):
        to = rem(own_ab + e, 4)
        send(astat.at[own_ab], astat.at[own_ab], ms_s, as_r.at[own_ab], ring_dev(y, z, l * 4 + to))

    @pl.when(native)
    def _():
        own_q = div(z, 2)
        bstat[own_q] = astat[own_ab]
        for d in (1, 7, 2, 6, 3, 5, 4):
            send(bstat.at[own_q], bstat.at[own_q], ms_s, bs_r.at[own_q], in_column(d))

    for i, e in enumerate((4, 2, 6)):
        slot = rem(xi + e, 8)
        wait(abuf.at[slot], a_r.at[slot])
        send(abuf.at[slot], abuf.at[slot], a_s.at[4 + i], a_r.at[slot], ring_dev(y, z, twin))

    for e in range(1, 4):
        wait(astat.at[rem(own_ab + e, 4)], as_r.at[rem(own_ab + e, 4)])

    def turn(slot):
        which = rem(slot, 4)
        mean, inv = astat[which, 0:1, :], astat[which, 1:2, :]
        normed = ((abuf[slot].astype(f32) - mean) * inv).astype(bf16)
        anorm[slot] = normed
        aturn[which, :, pl.ds(pl.multiple_of(div(slot, 4) * 512, 512), 512)] = normed.T

    for e in (0, 4, 2, 6):
        turn(rem(xi + e, 8))

    @pl.when(jnp.logical_not(native))
    def _():
        pass_b()

    for e in (0, 4, 2, 6):
        slot = rem(twin + e, 8)
        wait(abuf.at[slot], a_r.at[slot])
        turn(slot)

    def side(buf, k):
        return jnp.concatenate([buf[k * 4 + i] for i in range(4)], axis=1)

    over_cols = (((1,), (1,)), ((), ()))
    over_in = (((1,), (0,)), ((), ()))

    def block(t):
        ahead = jnp.where(native, (0, 2, 4, 6)[t], (7, 5, 3, 1)[t])
        return div(rem(z + ahead, 8), 2)

    def along_y(e):
        return dev(rem(y + e, 8), z, h, l, c)

    def rows_of(to):
        return pl.ds(pl.multiple_of(to * 64, 64), 64)

    def correlate(t):
        q = block(t)
        late = 1 - half
        wait(bbuf.at[late * 4 + q], b_r.at[late * 4 + q])
        if t == 2:
            wait(bbuf.at[half * 4 + q], b_r.at[half * 4 + q])

        @pl.when(jnp.logical_not(native) | (div(z, 2) != q))
        def _():
            wait(bstat.at[q], bs_r.at[q])

        mean, inv = bstat[q, 2:3, :], bstat[q, 3:4, :]
        right = jnp.concatenate([bbuf[q], bbuf[4 + q]], axis=0)
        right = ((right.astype(f32) - mean) * inv).astype(bf16)
        bnorm[q] = right[:512]
        bnorm[4 + q] = right[512:]
        left = jnp.concatenate([aturn[i] for i in range(4)], axis=0)
        part = lax.dot_general(left, right, over_in, preferred_element_type=f32)
        cwide[t] = part
        cnarrow[t] = part.astype(bf16)

        def go(e, to, slot, sem, lo=0, n=64):
            piece = cnarrow.at[t, pl.ds(pl.multiple_of(rem(y + e, 8) * 64 + lo, 32), n)]
            send(piece, crecv.at[t, slot, pl.ds(lo, n)], c_s.at[t], sem, along_y(to))

        if t in straight_c:
            for e in (4, 3, 5, 2, 6, 1, 7):
                go(e, e, e, c_r.at[t])
            return
        go(3, 1, 2, cp_r.at[t])
        go(5, 7, 3, cp_r.at[t])
        go(4, 6, 4, cp_r.at[t], 0, 32)
        go(4, 2, 5, cp_r.at[t], 32, 32)
        go(1, 1, 0, c_r.at[t])
        go(7, 7, 1, c_r.at[t])

    def pass_partial(t):
        if t in straight_c:
            return
        wait(crecv.at[t, pl.ds(0, 3)], cp_r.at[t])
        up = cwide[t, rows_of(rem(y + 2, 8)), :] + crecv[t, 2].astype(f32)
        cpass[t, 0, 0:32, :] = up[:32].astype(bf16)
        cpass[t, 0, 32:64, :] = (up[32:] + crecv[t, 5, 32:64, :].astype(f32)).astype(bf16)
        send(cpass.at[t, 0], crecv.at[t, 6], cp_s.at[t], c_r.at[t], along_y(2))
        down = cwide[t, rows_of(rem(y + 6, 8)), :] + crecv[t, 3].astype(f32)
        cpass[t, 1, 0:32, :] = (down[:32] + crecv[t, 4, 0:32, :].astype(f32)).astype(bf16)
        cpass[t, 1, 32:64, :] = down[32:].astype(bf16)
        send(cpass.at[t, 1], crecv.at[t, 7], cp_s.at[t], c_r.at[t], along_y(6))

    def differentiate(t):
        q = block(t)
        straight = t in straight_c
        wait(crecv.at[t, pl.ds(0, 7 if straight else 4)], c_r.at[t])
        corr = cwide[t, rows_of(y), :]
        for i in range(1, 8) if straight else (0, 1, 6, 7):
            corr = corr + crecv[t, i].astype(f32)
        corr = corr / pairs
        ctile[q] = corr
        row_ids = lax.broadcasted_iota(jnp.int32, corr.shape, 0)
        col_ids = lax.broadcasted_iota(jnp.int32, corr.shape, 1)
        here = jnp.where((z == 2 * q + l) & (div(y, 2) == h * 2 + c), rem(y, 2) * 64, 100000)
        grad = jnp.where(row_ids + here == col_ids, -2.0 * (1.0 - corr), 2.0 * off_weight * corr).astype(bf16)
        both = grad.astype(f32) * corr
        cols = jnp.sum(both, axis=0, keepdims=True)
        rows = jnp.sum(both.T, axis=0, keepdims=True)
        none = jnp.zeros_like(rows)
        rows = jnp.where(
            rem(y, 2) == 0, jnp.concatenate([rows, none], axis=1), jnp.concatenate([none, rows], axis=1)
        )
        terms = []
        for value in (cols, rows):
            high = value.astype(bf16).astype(f32)
            terms += [high, value - high]
        terms.append(jnp.zeros((12, 128), f32))
        gbuf[q, y, 0:64, :] = grad
        gbuf[q, y, 64:80, :] = jnp.concatenate(terms, axis=0).astype(bf16)
        if t in straight_g:
            for e in (4, 3, 5, 2, 6, 1, 7):
                send(gbuf.at[q, y], gbuf.at[q, y], g_s.at[t], g_r.at[t], along_y(e))
            return
        send(gbuf.at[q, y], gbuf.at[q, y], g_s.at[t], gp_r.at[t], along_y(2))
        send(gbuf.at[q, y], gbuf.at[q, y], g_s.at[t], gp_r.at[t], along_y(6))
        send(gbuf.at[q, y], gbuf.at[q, y], g_s.at[t], g_r.at[t], along_y(1))
        send(gbuf.at[q, y], gbuf.at[q, y], g_s.at[t], g_r.at[t], along_y(7))

    def pass_gradient(t):
        if t in straight_g:
            return
        q = block(t)
        wait(gbuf.at[q, pl.ds(0, 2)], gp_r.at[t])
        for frm, one, two, lo, n in ((6, 1, 2, 0, 48), (2, 7, 6, 48, 32)):
            item = gbuf.at[q, rem(y + frm, 8)]
            send(item, item, g_s.at[t], g_r.at[t], along_y(one))
            part = gbuf.at[q, rem(y + frm, 8), pl.ds(lo, n)]
            send(part, part, g_s.at[t], g_r.at[t], along_y(two))

    proj_a = [jnp.zeros((1, 128), f32)] * 4
    proj_b = []

    def take_gradient(t):
        q = block(t)
        wait(gbuf.at[q, pl.ds(0, 7 if t in straight_g else 5)], g_r.at[t])
        total = jnp.zeros((1, 128), f32)
        for i in range(8):
            gfull[q, i * 64 : (i + 1) * 64, :] = gbuf[q, i, 0:64, :]
            sums = gbuf[q, i, 64:80, :].astype(f32)
            total = total + (sums[0:1, :] + sums[1:2, :])
            proj_a[i // 2] = proj_a[i // 2] + (sums[2:3, :] + sums[3:4, :])
        proj_b.append(total)

    def back_columns(t):
        q = block(t)
        for j in range(2):
            k = l if j == 0 else 1 - l
            left = jnp.concatenate([anorm[k * 4 + i] for i in range(4)], axis=1)
            back = lax.dot_general(left, gfull[q], over_in, preferred_element_type=f32)
            back = back - bnorm[k * 4 + q].astype(f32) * proj_b[t]
            if t != 2:
                bkeep[min(t, 2), j] = back
            bsend[t, j] = back.astype(bf16)

            def act(off):
                src = bsend.at[t, j]
                sem = fb_s.at[t, j]
                if off in (1, 7):
                    i = 0 if off == 1 else 1
                    send(src, bback.at[i], sem, fb_r.at[i], in_column(off))
                if off in (3, 5):
                    p = 0 if off == 3 else 1
                    send(src, bfull.at[p], sem, ff_r.at[p], in_column((1, 7)[p]))
                if off == 4:
                    for p, d in enumerate((2, 6)):
                        rows = pl.ds(256 - p * 256, 256)
                        send(bsend.at[t, j, rows], bhalf.at[p, rows], sem, fh_r.at[p], in_column(d))

            @pl.when(native)
            def _():
                act(offs_on[t][j])

            @pl.when(jnp.logical_not(native))
            def _():
                act(offs_off[t][j])

    def pass_back(p):
        d = (2, 6)[p]
        keep = bkeep.at[jnp.where(native, (1, 2)[p], (2, 1)[p]), jnp.where(native, 0, 1)]
        rows = pl.ds(256 - p * 256, 256)
        wait(bfull.at[p], ff_r.at[p])
        wait(bhalf.at[p, rows], fh_r.at[p])
        one = slice(256 - p * 256, 512 - p * 256)
        other = slice(p * 256, 256 + p * 256)
        bpass[p, other, :] = (keep[other, :] + bfull[p, other, :].astype(f32)).astype(bf16)
        bpass[p, one, :] = (keep[one, :] + bfull[p, one, :].astype(f32) + bhalf[p, one, :].astype(f32)).astype(bf16)
        send(bpass.at[p], bback.at[2 + p], fbp_s.at[p], fb_r.at[2 + p], in_column(d))

    correlate(0)
    correlate(1)
    pass_partial(0)
    correlate(2)
    pass_partial(1)
    differentiate(0)
    correlate(3)
    pass_partial(2)
    differentiate(1)
    pass_gradient(0)
    pass_partial(3)
    differentiate(2)
    pass_gradient(1)
    take_gradient(0)
    back_columns(0)
    differentiate(3)
    pass_gradient(2)
    take_gradient(1)
    back_columns(1)
    pass_gradient(3)
    take_gradient(2)
    back_columns(2)

    take_gradient(3)
    whole_g = jnp.concatenate([gfull[q] for q in range(4)], axis=1)
    for k in range(2):
        back = lax.dot_general(side(bnorm, k), whole_g, over_cols, preferred_element_type=f32)
        for i in range(4):
            less = back[:, i * 128 : (i + 1) * 128] - anorm[k * 4 + i].astype(f32) * proj_a[i]
            akeep[k * 4 + i] = less
            asend[k * 4 + i] = less.astype(bf16)
    chip = l * 2 + h
    for e in (2, 1, 3, 0):
        to = rem(chip + e, 4)
        send(asend.at[to * 2 + 1 - c], ain.at[to], fd_s.at[e], fd_r.at[to], ring_dev(y, z, twin))

    @pl.when(native)
    def _():
        pass_back(0)

    @pl.when(jnp.logical_not(native))
    def _():
        pass_back(1)

    back_columns(3)

    @pl.when(native)
    def _():
        pass_back(1)

    @pl.when(jnp.logical_not(native))
    def _():
        pass_back(0)

    for q in range(4):
        stay = at_home & (div(y, 2) == q)

        @pl.when(stay)
        def _(q=q):
            corrb[c, rem(y, 2)] = ctile[q]

        @pl.when(jnp.logical_not(stay))
        def _(q=q):
            send(ctile.at[q], corrb.at[c, rem(y, 2)], o_s.at[q], o_r.at[c, rem(y, 2)], corr_to(q))

    for e in (2, 1, 3, 0):
        to = rem(chip + e, 4)
        wait(ain.at[to], fd_r.at[to])
        summed = (akeep[to * 2 + c] + ain[to].astype(f32)).astype(bf16)
        if e:
            apass[e] = summed
            send(apass.at[e], aback.at[chip], fa_s.at[e], fa_r.at[chip], ring_dev(y, z, to * 2 + c))
        else:
            aback[chip] = summed

    for k in range(2):
        for p in range(2):
            @pl.when(jnp.logical_not(at_home & (c == k) & (rem(y, 2) == p)))
            def _(k=k, p=p):
                wait(corrb.at[k, p], o_r.at[k, p])

            co[p * 64 : (p + 1) * 64, k * 128 : (k + 1) * 128] = corrb[k, p]

    acc = bkeep[0, jnp.where(native, 0, 1)]
    for i in range(4):
        wait(bback.at[i], fb_r.at[i])
        acc = acc + bback[i].astype(f32)

    @pl.when(native)
    def _():
        gb[...] = (acc * inv_b).astype(bf16)

    @pl.when(jnp.logical_not(native))
    def _():
        wait(bown, bx_s)
        bown[...] = acc.astype(bf16)
        send(bown, bcross, bc_s, bc_r, dev(y, rem(z + 7, 8), h, 1 - l, c))

    for e in range(1, 4):
        frm = rem(chip + e, 4)
        wait(aback.at[frm], fa_r.at[frm])
    acc = aback[0].astype(f32)
    for i in range(1, 4):
        acc = acc + aback[i].astype(f32)
    ga[...] = (acc * inv_a).astype(bf16)

    @pl.when(jnp.logical_not(native))
    def _():
        wait(bcross, bc_r)
        gb[...] = (bcross[...].astype(f32) * inv_b).astype(bf16)

    @pl.when(native)
    def _():
        wait(stats.at[pl.ds(0, 10)], ms_s)

    @pl.when(jnp.logical_not(native))
    def _():
        wait(stats.at[pl.ds(0, 3)], ms_s)

    wait(stats.at[pl.ds(0, 15)], st_s)
    for i in range(7):
        wait(abuf.at[xi], a_s.at[i])
    for e in range(4):
        wait(asend.at[0], fd_s.at[e])
        if e:
            wait(apass.at[e], fa_s.at[e])

    @pl.when(jnp.logical_not(native))
    def _():
        wait(bown, bc_s)

    for i in range(4):
        wait(bbuf.at[0], b_s.at[i])
    for p in range(2):
        wait(bbuf.at[0], bp_s.at[p, 0])
        wait(bbuf.at[0, pl.ds(0, 256)], bp_s.at[p, 1])
        wait(bpass.at[p], fbp_s.at[p])

    for t in range(4):
        wait(crecv.at[t, pl.ds(0, 7 if t in straight_c else 5)], c_s.at[t])
        if t not in straight_c:
            wait(crecv.at[t, pl.ds(0, 2)], cp_s.at[t])
        wait(gbuf.at[t, pl.ds(0, 7)], g_s.at[t])

        @pl.when(jnp.logical_not(at_home & (div(y, 2) == t)))
        def _(t=t):
            wait(ctile.at[t], o_s.at[t])

        for j in range(2):
            goes_on = offs_on[t][j] not in (0, 2, 6)
            goes_off = offs_off[t][j] not in (0, 2, 6)
            if goes_on and goes_off:
                wait(bsend.at[t, j], fb_s.at[t, j])
            elif goes_on:
                @pl.when(native)
                def _(t=t, j=j):
                    wait(bsend.at[t, j], fb_s.at[t, j])
            elif goes_off:
                @pl.when(jnp.logical_not(native))
                def _(t=t, j=j):
                    wait(bsend.at[t, j], fb_s.at[t, j])


def body(view_a, view_b):
    rows, cols = view_a.shape
    pairs = rows * lax.axis_size("batch")
    vmem = pl.BlockSpec(memory_space=pltpu.VMEM)
    dma = pltpu.SemaphoreType.DMA

    def call(*args):
        return kernel(float(pairs), *args)

    results = pl.pallas_call(
        call,
        name="barlow",
        out_shape=(
            jax.ShapeDtypeStruct((rows, cols), bf16),
            jax.ShapeDtypeStruct((rows, cols), bf16),
            jax.ShapeDtypeStruct((128, 256), f32),
        ),
        in_specs=[pl.BlockSpec(memory_space=pltpu.HBM)] * 2,
        out_specs=(vmem, vmem, vmem),
        scratch_shapes=[
            pltpu.VMEM((rows, cols), bf16),
            pltpu.VMEM((rows, cols), bf16),
            dma((2,)),
            pltpu.VMEM((8, 128), f32),
            pltpu.VMEM((16, 8, 128), f32),
            pltpu.VMEM((4, 8, 128), f32),
            pltpu.VMEM((4, 8, 128), f32),
            pltpu.VMEM((8, rows, 128), bf16),
            pltpu.VMEM((8, rows, 128), bf16),
            pltpu.VMEM((8, rows, 128), bf16),
            pltpu.VMEM((8, rows, 128), bf16),
            pltpu.VMEM((4, 128, 1024), bf16),
            pltpu.VMEM((4, 512, 128), f32),
            pltpu.VMEM((4, 512, 128), bf16),
            pltpu.VMEM((4, 8, 64, 128), bf16),
            pltpu.VMEM((4, 2, 64, 128), bf16),
            pltpu.VMEM((4, 64, 128), f32),
            pltpu.VMEM((2, 2, 64, 128), f32),
            pltpu.VMEM((4, 8, 80, 128), bf16),
            pltpu.VMEM((4, 512, 128), bf16),
            pltpu.VMEM((4, 2, rows, 128), bf16),
            pltpu.VMEM((3, 2, rows, 128), f32),
            pltpu.VMEM((2, rows, 128), bf16),
            pltpu.VMEM((2, rows, 128), bf16),
            pltpu.VMEM((2, rows, 128), bf16),
            pltpu.VMEM((4, rows, 128), bf16),
            pltpu.VMEM((rows, 128), bf16),
            pltpu.VMEM((rows, 128), bf16),
            pltpu.VMEM((8, rows, 128), bf16),
            pltpu.VMEM((8, rows, 128), f32),
            pltpu.VMEM((4, rows, 128), bf16),
            pltpu.VMEM((4, rows, 128), bf16),
            pltpu.VMEM((4, rows, 128), bf16),
            dma, dma, dma, dma((4,)), dma((4,)),
            dma((7,)), dma((8,)), dma((4,)), dma((8,)), dma((2, 2)),
            dma((4,)), dma((4,)), dma((4,)), dma((4,)), dma((4,)), dma((2, 2)), dma((4,)), dma((4,)), dma((4,)),
            dma((4, 2)), dma((2,)), dma((2,)), dma((2,)), dma((4,)),
            dma((4,)), dma((4,)), dma((4,)), dma((4,)), dma, dma, dma, dma,
        ],
        compiler_params=pltpu.CompilerParams(
            collective_id=0, has_side_effects=True, vmem_limit_bytes=60 * 2**20
        ),
    )(view_a, view_b)

    def place(grad_a, grad_b, corr, out_a, out_b, out_c, sems):
        copies = [
            pltpu.make_async_copy(src, dst, sems.at[i])
            for i, (src, dst) in enumerate(((grad_a, out_a), (grad_b, out_b), (corr, out_c)))
        ]
        for copy in copies:
            copy.start()
        for copy in copies:
            copy.wait()

    anywhere = pl.BlockSpec(memory_space=pl.ANY)
    return pl.pallas_call(
        place,
        name="place",
        out_shape=tuple(jax.ShapeDtypeStruct(r.shape, r.dtype) for r in results),
        in_specs=[vmem] * 3,
        out_specs=(anywhere,) * 3,
        scratch_shapes=[dma((3,))],
    )(*results)


def solution(mesh):
    return jax.shard_map(
        body,
        mesh=mesh,
        in_specs=(P("batch", "feat"), P("batch", "feat")),
        out_specs=(P("batch", "feat"), P("batch", "feat"), P("feat", "batch")),
        check_vma=False,
    )
```

```python
import jax
import jax.numpy as jnp
from jax import lax
from jax.experimental import pallas as pl
from jax.experimental.pallas import tpu as pltpu
from jax.sharding import PartitionSpec as P

MESH = pl.DeviceIdType.MESH
epsilon = 1e-05
off_weight = 0.0051
f32 = jnp.float32
bf16 = jnp.bfloat16


def div(a, n):
    return lax.div(a, jnp.int32(n))


def rem(a, n):
    return lax.rem(a, jnp.int32(n))


straight_c = ()
straight_g = ()

offs_on = ((0, 1), (2, 3), (4, 5), (6, 7))
offs_off = ((7, 0), (5, 6), (3, 4), (1, 2))


def kernel(
    pairs,
    view_a, view_b,
    ga, gb, co,
    va, vb, in_s,
    stat_own, stats, astat, bstat, abuf, bbuf, anorm, bnorm, aturn, cwide, cnarrow, crecv, cpass, ctile, corrb,
    gbuf, gfull, bsend, bkeep, bfull, bhalf, bpass, bback, bown, bcross, asend, akeep, ain, apass, aback,
    st_s, st_r, ms_s, as_r, bs_r, a_s, a_r, b_s, b_r, bp_s, c_s, cp_s, cp_r, c_r, o_s, o_r, g_s, gp_r, g_r,
    fb_s, fbp_s, ff_r, fh_r, fb_r, fd_s, fd_r, fa_s, fa_r, bx_r, bx_s, bc_r, bc_s,
):
    b = lax.axis_index("batch")
    f = lax.axis_index("feat")
    y, l = div(b, 2), rem(b, 2)
    z, h, c = div(f, 4), rem(div(f, 2), 2), rem(f, 2)
    xi = l * 4 + h * 2 + c

    def dev(y_, z_, h_, l_, c_):
        return (y_ * 2 + l_, z_ * 4 + h_ * 2 + c_)

    def ring_dev(y_, z_, xi_):
        return dev(y_, z_, rem(div(xi_, 2), 2), div(xi_, 4), rem(xi_, 2))

    def send(src, dst, s_sem, r_sem, to):
        pltpu.make_async_remote_copy(
            src_ref=src, dst_ref=dst, send_sem=s_sem, recv_sem=r_sem, device_id=to, device_id_type=MESH
        ).start()

    def wait(ref, sem):
        pltpu.make_async_copy(ref, ref, sem).wait()

    def loop(lo, hi, fn):
        def step(i, carry):
            fn(i)
            return carry

        lax.fori_loop(lo, hi, step, 0)

    def corr_to(q):
        return dev(2 * q + l, z, div(y, 4), h, rem(div(y, 2), 2))

    def corr_from(k, p):
        return dev(h * 4 + c * 2 + p, z, l, rem(y, 2), k)

    at_home = (rem(y, 2) == l) & (h == l) & (div(y, 2) == h * 2 + c)

    pltpu.make_async_copy(view_a, va, in_s.at[0]).start()
    pltpu.make_async_copy(view_b, vb, in_s.at[1]).start()

    barrier = pltpu.get_barrier_semaphore()

    def greet(to):
        pl.semaphore_signal(barrier, inc=1, device_id=to, device_id_type=MESH)

    loop(1, 16, lambda e: greet((rem(b + e, 16), f)))
    loop(1, 8, lambda e: greet(ring_dev(y, z, rem(xi + e, 8))))
    loop(1, 8, lambda e: greet(dev(y, rem(z + e, 8), h, l, c)))
    loop(1, 8, lambda e: greet(dev(y, rem(z + e, 8), h, 1 - l, c)))
    for q in range(4):
        @pl.when(jnp.logical_not(at_home & (div(y, 2) == q)))
        def _(q=q):
            greet(corr_to(q))

        @pl.when(jnp.logical_not(at_home & (c == q // 2) & (rem(y, 2) == q % 2)))
        def _(q=q):
            greet(corr_from(q // 2, q % 2))

    wait(va, in_s.at[0])
    wait(vb, in_s.at[1])
    wide_a = va[...].astype(f32)
    wide_b = vb[...].astype(f32)
    stat_own[0:1, :] = jnp.sum(wide_a, axis=0, keepdims=True)
    stat_own[1:2, :] = jnp.sum(wide_a * wide_a, axis=0, keepdims=True)
    stat_own[2:3, :] = jnp.sum(wide_b, axis=0, keepdims=True)
    stat_own[3:4, :] = jnp.sum(wide_b * wide_b, axis=0, keepdims=True)
    stat_own[4:8, :] = jnp.zeros((4, 128), f32)
    stats[b] = stat_own[...]

    pl.semaphore_wait(barrier, 15 + 7 + 7 + 7 + 8 - 2 * at_home.astype(jnp.int32))

    loop(1, 16, lambda e: send(stat_own, stats.at[b], st_s, st_r, (rem(b + e, 16), f)))

    half = rem(z, 2)
    native = half == l
    twin = xi + 1 - 2 * c

    def in_column(d):
        return dev(y, rem(z + d, 8), h, l, c)

    def slot_at(d):
        place = rem(z + d, 8)
        on = rem(rem(place, 2) + l + 1, 2)
        return (on * l + (1 - on) * (1 - l)) * 4 + div(rem(place + 7 + on, 8), 2)

    def spread_b():
        slot = slot_at(0)
        for i, d in enumerate((2, 6, 1, 7)):
            send(bbuf.at[slot], bbuf.at[slot], b_s.at[i], b_r.at[slot], in_column(d))

    def pass_b():
        for p, (frm, one, two) in enumerate(((6, 1, 2), (2, 7, 6))):
            slot = slot_at(frm)
            wait(bbuf.at[slot], b_r.at[slot])
            send(bbuf.at[slot], bbuf.at[slot], bp_s.at[p, 0], b_r.at[slot], in_column(one))
            part = bbuf.at[slot, pl.ds(p * 256, 256)]
            send(part, part, bp_s.at[p, 1], b_r.at[slot], in_column(two))

    @pl.when(native)
    def _():
        bbuf[slot_at(0)] = vb[...]
        spread_b()

    @pl.when(jnp.logical_not(native))
    def _():
        bown[...] = vb[...]
        slot = l * 4 + div(z, 2)
        send(bown, bbuf.at[slot], bx_s, bx_r, dev(y, rem(z + 1, 8), h, half, c))

    abuf[xi] = va[...]
    for i, e in enumerate((4, 2, 6)):
        send(abuf.at[xi], abuf.at[xi], a_s.at[i], a_r.at[xi], ring_dev(y, z, rem(xi + e, 8)))
    send(abuf.at[xi], abuf.at[xi], a_s.at[3], a_r.at[xi], ring_dev(y, z, twin))

    @pl.when(native)
    def _():
        pass_b()

    @pl.when(jnp.logical_not(native))
    def _():
        wait(bbuf.at[slot_at(0)], bx_r)
        spread_b()

    wait(stats.at[pl.ds(0, 15)], st_r)
    total = stats[0]
    for i in range(1, 16):
        total = total + stats[i]
    total = total / pairs
    mean_a, mean_b = total[0:1, :], total[2:3, :]
    inv_a = lax.rsqrt(total[1:2, :] - mean_a * mean_a + epsilon)
    inv_b = lax.rsqrt(total[3:4, :] - mean_b * mean_b + epsilon)
    own_ab = h * 2 + c
    astat[own_ab] = jnp.concatenate([mean_a, inv_a, mean_b, inv_b, jnp.zeros((4, 128), f32)], axis=0)
    for e in range(1, 4):
        to = rem(own_ab + e, 4)
        send(astat.at[own_ab], astat.at[own_ab], ms_s, as_r.at[own_ab], ring_dev(y, z, l * 4 + to))

    @pl.when(native)
    def _():
        own_q = div(z, 2)
        bstat[own_q] = astat[own_ab]
        for d in (1, 7, 2, 6, 3, 5, 4):
            send(bstat.at[own_q], bstat.at[own_q], ms_s, bs_r.at[own_q], in_column(d))

    for i, e in enumerate((4, 2, 6)):
        slot = rem(xi + e, 8)
        wait(abuf.at[slot], a_r.at[slot])
        send(abuf.at[slot], abuf.at[slot], a_s.at[4 + i], a_r.at[slot], ring_dev(y, z, twin))

    for e in range(1, 4):
        wait(astat.at[rem(own_ab + e, 4)], as_r.at[rem(own_ab + e, 4)])

    def turn(slot):
        which = rem(slot, 4)
        mean, inv = astat[which, 0:1, :], astat[which, 1:2, :]
        normed = ((abuf[slot].astype(f32) - mean) * inv).astype(bf16)
        anorm[slot] = normed
        aturn[which, :, pl.ds(pl.multiple_of(div(slot, 4) * 512, 512), 512)] = normed.T

    for e in (0, 4, 2, 6):
        turn(rem(xi + e, 8))

    @pl.when(jnp.logical_not(native))
    def _():
        pass_b()

    for e in (0, 4, 2, 6):
        slot = rem(twin + e, 8)
        wait(abuf.at[slot], a_r.at[slot])
        turn(slot)

    def side(buf, k):
        return jnp.concatenate([buf[k * 4 + i] for i in range(4)], axis=1)

    over_cols = (((1,), (1,)), ((), ()))
    over_in = (((1,), (0,)), ((), ()))

    def block(t):
        ahead = jnp.where(native, (0, 2, 4, 6)[t], (7, 5, 3, 1)[t])
        return div(rem(z + ahead, 8), 2)

    def along_y(e):
        return dev(rem(y + e, 8), z, h, l, c)

    def rows_of(to):
        return pl.ds(pl.multiple_of(to * 64, 64), 64)

    def correlate(t):
        q = block(t)
        late = 1 - half
        wait(bbuf.at[late * 4 + q], b_r.at[late * 4 + q])
        if t == 2:
            wait(bbuf.at[half * 4 + q], b_r.at[half * 4 + q])

        @pl.when(jnp.logical_not(native) | (div(z, 2) != q))
        def _():
            wait(bstat.at[q], bs_r.at[q])

        mean, inv = bstat[q, 2:3, :], bstat[q, 3:4, :]
        right = jnp.concatenate([bbuf[q], bbuf[4 + q]], axis=0)
        right = ((right.astype(f32) - mean) * inv).astype(bf16)
        bnorm[q] = right[:512]
        bnorm[4 + q] = right[512:]
        left = jnp.concatenate([aturn[i] for i in range(4)], axis=0)
        part = lax.dot_general(left, right, over_in, preferred_element_type=f32)
        cwide[t] = part
        cnarrow[t] = part.astype(bf16)

        def go(e, to, slot, sem, lo=0, n=64):
            piece = cnarrow.at[t, pl.ds(pl.multiple_of(rem(y + e, 8) * 64 + lo, 32), n)]
            send(piece, crecv.at[t, slot, pl.ds(lo, n)], c_s.at[t], sem, along_y(to))

        if t in straight_c:
            for e in (4, 3, 5, 2, 6, 1, 7):
                go(e, e, e, c_r.at[t])
            return
        go(3, 1, 2, cp_r.at[t])
        go(5, 7, 3, cp_r.at[t])
        go(4, 6, 4, cp_r.at[t], 0, 32)
        go(4, 2, 5, cp_r.at[t], 32, 32)
        go(1, 1, 0, c_r.at[t])
        go(7, 7, 1, c_r.at[t])

    def pass_partial(t):
        if t in straight_c:
            return
        wait(crecv.at[t, pl.ds(0, 3)], cp_r.at[t])
        up = cwide[t, rows_of(rem(y + 2, 8)), :] + crecv[t, 2].astype(f32)
        cpass[t, 0, 0:32, :] = up[:32].astype(bf16)
        cpass[t, 0, 32:64, :] = (up[32:] + crecv[t, 5, 32:64, :].astype(f32)).astype(bf16)
        send(cpass.at[t, 0], crecv.at[t, 6], cp_s.at[t], c_r.at[t], along_y(2))
        down = cwide[t, rows_of(rem(y + 6, 8)), :] + crecv[t, 3].astype(f32)
        cpass[t, 1, 0:32, :] = (down[:32] + crecv[t, 4, 0:32, :].astype(f32)).astype(bf16)
        cpass[t, 1, 32:64, :] = down[32:].astype(bf16)
        send(cpass.at[t, 1], crecv.at[t, 7], cp_s.at[t], c_r.at[t], along_y(6))

    def differentiate(t):
        q = block(t)
        straight = t in straight_c
        wait(crecv.at[t, pl.ds(0, 7 if straight else 4)], c_r.at[t])
        corr = cwide[t, rows_of(y), :]
        for i in range(1, 8) if straight else (0, 1, 6, 7):
            corr = corr + crecv[t, i].astype(f32)
        corr = corr / pairs
        ctile[q] = corr
        row_ids = lax.broadcasted_iota(jnp.int32, corr.shape, 0)
        col_ids = lax.broadcasted_iota(jnp.int32, corr.shape, 1)
        here = jnp.where((z == 2 * q + l) & (div(y, 2) == h * 2 + c), rem(y, 2) * 64, 100000)
        grad = jnp.where(row_ids + here == col_ids, -2.0 * (1.0 - corr), 2.0 * off_weight * corr).astype(bf16)
        both = grad.astype(f32) * corr
        cols = jnp.sum(both, axis=0, keepdims=True)
        rows = jnp.sum(both.T, axis=0, keepdims=True)
        none = jnp.zeros_like(rows)
        rows = jnp.where(
            rem(y, 2) == 0, jnp.concatenate([rows, none], axis=1), jnp.concatenate([none, rows], axis=1)
        )
        terms = []
        for value in (cols, rows):
            high = value.astype(bf16).astype(f32)
            terms += [high, value - high]
        terms.append(jnp.zeros((12, 128), f32))
        gbuf[q, y, 0:64, :] = grad
        gbuf[q, y, 64:80, :] = jnp.concatenate(terms, axis=0).astype(bf16)
        if t in straight_g:
            for e in (4, 3, 5, 2, 6, 1, 7):
                send(gbuf.at[q, y], gbuf.at[q, y], g_s.at[t], g_r.at[t], along_y(e))
            return
        send(gbuf.at[q, y], gbuf.at[q, y], g_s.at[t], gp_r.at[t], along_y(2))
        send(gbuf.at[q, y], gbuf.at[q, y], g_s.at[t], gp_r.at[t], along_y(6))
        send(gbuf.at[q, y], gbuf.at[q, y], g_s.at[t], g_r.at[t], along_y(1))
        send(gbuf.at[q, y], gbuf.at[q, y], g_s.at[t], g_r.at[t], along_y(7))

    def pass_gradient(t):
        if t in straight_g:
            return
        q = block(t)
        wait(gbuf.at[q, pl.ds(0, 2)], gp_r.at[t])
        for frm, one, two, lo, n in ((6, 1, 2, 0, 48), (2, 7, 6, 48, 32)):
            item = gbuf.at[q, rem(y + frm, 8)]
            send(item, item, g_s.at[t], g_r.at[t], along_y(one))
            part = gbuf.at[q, rem(y + frm, 8), pl.ds(lo, n)]
            send(part, part, g_s.at[t], g_r.at[t], along_y(two))

    proj_a = [jnp.zeros((1, 128), f32)] * 4
    proj_b = []

    def take_gradient(t):
        q = block(t)
        wait(gbuf.at[q, pl.ds(0, 7 if t in straight_g else 5)], g_r.at[t])
        total = jnp.zeros((1, 128), f32)
        for i in range(8):
            gfull[q, i * 64 : (i + 1) * 64, :] = gbuf[q, i, 0:64, :]
            sums = gbuf[q, i, 64:80, :].astype(f32)
            total = total + (sums[0:1, :] + sums[1:2, :])
            proj_a[i // 2] = proj_a[i // 2] + (sums[2:3, :] + sums[3:4, :])
        proj_b.append(total)

    def back_columns(t):
        q = block(t)
        for j in range(2):
            k = l if j == 0 else 1 - l
            left = jnp.concatenate([anorm[k * 4 + i] for i in range(4)], axis=1)
            back = lax.dot_general(left, gfull[q], over_in, preferred_element_type=f32)
            back = back - bnorm[k * 4 + q].astype(f32) * proj_b[t]
            if t != 2:
                bkeep[min(t, 2), j] = back
            bsend[t, j] = back.astype(bf16)

            def act(off):
                src = bsend.at[t, j]
                sem = fb_s.at[t, j]
                if off in (1, 7):
                    i = 0 if off == 1 else 1
                    send(src, bback.at[i], sem, fb_r.at[i], in_column(off))
                if off in (3, 5):
                    p = 0 if off == 3 else 1
                    send(src, bfull.at[p], sem, ff_r.at[p], in_column((1, 7)[p]))
                if off == 4:
                    for p, d in enumerate((2, 6)):
                        rows = pl.ds(256 - p * 256, 256)
                        send(bsend.at[t, j, rows], bhalf.at[p, rows], sem, fh_r.at[p], in_column(d))

            @pl.when(native)
            def _():
                act(offs_on[t][j])

            @pl.when(jnp.logical_not(native))
            def _():
                act(offs_off[t][j])

    def pass_back(p):
        d = (2, 6)[p]
        keep = bkeep.at[jnp.where(native, (1, 2)[p], (2, 1)[p]), jnp.where(native, 0, 1)]
        rows = pl.ds(256 - p * 256, 256)
        wait(bfull.at[p], ff_r.at[p])
        wait(bhalf.at[p, rows], fh_r.at[p])
        one = slice(256 - p * 256, 512 - p * 256)
        other = slice(p * 256, 256 + p * 256)
        bpass[p, other, :] = (keep[other, :] + bfull[p, other, :].astype(f32)).astype(bf16)
        bpass[p, one, :] = (keep[one, :] + bfull[p, one, :].astype(f32) + bhalf[p, one, :].astype(f32)).astype(bf16)
        send(bpass.at[p], bback.at[2 + p], fbp_s.at[p], fb_r.at[2 + p], in_column(d))

    correlate(0)
    correlate(1)
    pass_partial(0)
    correlate(2)
    pass_partial(1)
    differentiate(0)
    correlate(3)
    pass_partial(2)
    differentiate(1)
    pass_gradient(0)
    pass_partial(3)
    differentiate(2)
    pass_gradient(1)
    take_gradient(0)
    back_columns(0)
    differentiate(3)
    pass_gradient(2)
    take_gradient(1)
    back_columns(1)
    pass_gradient(3)
    take_gradient(2)
    back_columns(2)

    take_gradient(3)
    back_columns(3)
    whole_g = jnp.concatenate([gfull[q] for q in range(4)], axis=1)
    for k in range(2):
        back = lax.dot_general(side(bnorm, k), whole_g, over_cols, preferred_element_type=f32)
        for i in range(4):
            less = back[:, i * 128 : (i + 1) * 128] - anorm[k * 4 + i].astype(f32) * proj_a[i]
            akeep[k * 4 + i] = less
            asend[k * 4 + i] = less.astype(bf16)
    chip = l * 2 + h
    for e in (2, 1, 3, 0):
        to = rem(chip + e, 4)
        send(asend.at[to * 2 + 1 - c], ain.at[to], fd_s.at[e], fd_r.at[to], ring_dev(y, z, twin))

    @pl.when(native)
    def _():
        pass_back(0)

    @pl.when(jnp.logical_not(native))
    def _():
        pass_back(1)

    @pl.when(native)
    def _():
        pass_back(1)

    @pl.when(jnp.logical_not(native))
    def _():
        pass_back(0)

    for q in range(4):
        stay = at_home & (div(y, 2) == q)

        @pl.when(stay)
        def _(q=q):
            corrb[c, rem(y, 2)] = ctile[q]

        @pl.when(jnp.logical_not(stay))
        def _(q=q):
            send(ctile.at[q], corrb.at[c, rem(y, 2)], o_s.at[q], o_r.at[c, rem(y, 2)], corr_to(q))

    for e in (2, 1, 3, 0):
        to = rem(chip + e, 4)
        wait(ain.at[to], fd_r.at[to])
        summed = (akeep[to * 2 + c] + ain[to].astype(f32)).astype(bf16)
        if e:
            apass[e] = summed
            send(apass.at[e], aback.at[chip], fa_s.at[e], fa_r.at[chip], ring_dev(y, z, to * 2 + c))
        else:
            aback[chip] = summed

    for k in range(2):
        for p in range(2):
            @pl.when(jnp.logical_not(at_home & (c == k) & (rem(y, 2) == p)))
            def _(k=k, p=p):
                wait(corrb.at[k, p], o_r.at[k, p])

            co[p * 64 : (p + 1) * 64, k * 128 : (k + 1) * 128] = corrb[k, p]

    acc = bkeep[0, jnp.where(native, 0, 1)]
    for i in range(4):
        wait(bback.at[i], fb_r.at[i])
        acc = acc + bback[i].astype(f32)

    @pl.when(native)
    def _():
        gb[...] = (acc * inv_b).astype(bf16)

    @pl.when(jnp.logical_not(native))
    def _():
        wait(bown, bx_s)
        bown[...] = acc.astype(bf16)
        send(bown, bcross, bc_s, bc_r, dev(y, rem(z + 7, 8), h, 1 - l, c))

    for e in range(1, 4):
        frm = rem(chip + e, 4)
        wait(aback.at[frm], fa_r.at[frm])
    acc = aback[0].astype(f32)
    for i in range(1, 4):
        acc = acc + aback[i].astype(f32)
    ga[...] = (acc * inv_a).astype(bf16)

    @pl.when(jnp.logical_not(native))
    def _():
        wait(bcross, bc_r)
        gb[...] = (bcross[...].astype(f32) * inv_b).astype(bf16)

    @pl.when(native)
    def _():
        wait(stats.at[pl.ds(0, 10)], ms_s)

    @pl.when(jnp.logical_not(native))
    def _():
        wait(stats.at[pl.ds(0, 3)], ms_s)

    wait(stats.at[pl.ds(0, 15)], st_s)
    for i in range(7):
        wait(abuf.at[xi], a_s.at[i])
    for e in range(4):
        wait(asend.at[0], fd_s.at[e])
        if e:
            wait(apass.at[e], fa_s.at[e])

    @pl.when(jnp.logical_not(native))
    def _():
        wait(bown, bc_s)

    for i in range(4):
        wait(bbuf.at[0], b_s.at[i])
    for p in range(2):
        wait(bbuf.at[0], bp_s.at[p, 0])
        wait(bbuf.at[0, pl.ds(0, 256)], bp_s.at[p, 1])
        wait(bpass.at[p], fbp_s.at[p])

    for t in range(4):
        wait(crecv.at[t, pl.ds(0, 7 if t in straight_c else 5)], c_s.at[t])
        if t not in straight_c:
            wait(crecv.at[t, pl.ds(0, 2)], cp_s.at[t])
        wait(gbuf.at[t, pl.ds(0, 7)], g_s.at[t])

        @pl.when(jnp.logical_not(at_home & (div(y, 2) == t)))
        def _(t=t):
            wait(ctile.at[t], o_s.at[t])

        for j in range(2):
            goes_on = offs_on[t][j] not in (0, 2, 6)
            goes_off = offs_off[t][j] not in (0, 2, 6)
            if goes_on and goes_off:
                wait(bsend.at[t, j], fb_s.at[t, j])
            elif goes_on:
                @pl.when(native)
                def _(t=t, j=j):
                    wait(bsend.at[t, j], fb_s.at[t, j])
            elif goes_off:
                @pl.when(jnp.logical_not(native))
                def _(t=t, j=j):
                    wait(bsend.at[t, j], fb_s.at[t, j])


def body(view_a, view_b):
    rows, cols = view_a.shape
    pairs = rows * lax.axis_size("batch")
    vmem = pl.BlockSpec(memory_space=pltpu.VMEM)
    dma = pltpu.SemaphoreType.DMA

    def call(*args):
        return kernel(float(pairs), *args)

    results = pl.pallas_call(
        call,
        name="barlow",
        out_shape=(
            jax.ShapeDtypeStruct((rows, cols), bf16),
            jax.ShapeDtypeStruct((rows, cols), bf16),
            jax.ShapeDtypeStruct((128, 256), f32),
        ),
        in_specs=[pl.BlockSpec(memory_space=pltpu.HBM)] * 2,
        out_specs=(vmem, vmem, vmem),
        scratch_shapes=[
            pltpu.VMEM((rows, cols), bf16),
            pltpu.VMEM((rows, cols), bf16),
            dma((2,)),
            pltpu.VMEM((8, 128), f32),
            pltpu.VMEM((16, 8, 128), f32),
            pltpu.VMEM((4, 8, 128), f32),
            pltpu.VMEM((4, 8, 128), f32),
            pltpu.VMEM((8, rows, 128), bf16),
            pltpu.VMEM((8, rows, 128), bf16),
            pltpu.VMEM((8, rows, 128), bf16),
            pltpu.VMEM((8, rows, 128), bf16),
            pltpu.VMEM((4, 128, 1024), bf16),
            pltpu.VMEM((4, 512, 128), f32),
            pltpu.VMEM((4, 512, 128), bf16),
            pltpu.VMEM((4, 8, 64, 128), bf16),
            pltpu.VMEM((4, 2, 64, 128), bf16),
            pltpu.VMEM((4, 64, 128), f32),
            pltpu.VMEM((2, 2, 64, 128), f32),
            pltpu.VMEM((4, 8, 80, 128), bf16),
            pltpu.VMEM((4, 512, 128), bf16),
            pltpu.VMEM((4, 2, rows, 128), bf16),
            pltpu.VMEM((3, 2, rows, 128), f32),
            pltpu.VMEM((2, rows, 128), bf16),
            pltpu.VMEM((2, rows, 128), bf16),
            pltpu.VMEM((2, rows, 128), bf16),
            pltpu.VMEM((4, rows, 128), bf16),
            pltpu.VMEM((rows, 128), bf16),
            pltpu.VMEM((rows, 128), bf16),
            pltpu.VMEM((8, rows, 128), bf16),
            pltpu.VMEM((8, rows, 128), f32),
            pltpu.VMEM((4, rows, 128), bf16),
            pltpu.VMEM((4, rows, 128), bf16),
            pltpu.VMEM((4, rows, 128), bf16),
            dma, dma, dma, dma((4,)), dma((4,)),
            dma((7,)), dma((8,)), dma((4,)), dma((8,)), dma((2, 2)),
            dma((4,)), dma((4,)), dma((4,)), dma((4,)), dma((4,)), dma((2, 2)), dma((4,)), dma((4,)), dma((4,)),
            dma((4, 2)), dma((2,)), dma((2,)), dma((2,)), dma((4,)),
            dma((4,)), dma((4,)), dma((4,)), dma((4,)), dma, dma, dma, dma,
        ],
        compiler_params=pltpu.CompilerParams(
            collective_id=0, has_side_effects=True, vmem_limit_bytes=60 * 2**20
        ),
    )(view_a, view_b)

    def place(grad_a, grad_b, corr, out_a, out_b, out_c, sems):
        copies = [
            pltpu.make_async_copy(src, dst, sems.at[i])
            for i, (src, dst) in enumerate(((grad_a, out_a), (grad_b, out_b), (corr, out_c)))
        ]
        for copy in copies:
            copy.start()
        for copy in copies:
            copy.wait()

    anywhere = pl.BlockSpec(memory_space=pl.ANY)
    return pl.pallas_call(
        place,
        name="place",
        out_shape=tuple(jax.ShapeDtypeStruct(r.shape, r.dtype) for r in results),
        in_specs=[vmem] * 3,
        out_specs=(anywhere,) * 3,
        scratch_shapes=[dma((3,))],
    )(*results)


def solution(mesh):
    return jax.shard_map(
        body,
        mesh=mesh,
        in_specs=(P("batch", "feat"), P("batch", "feat")),
        out_specs=(P("batch", "feat"), P("batch", "feat"), P("feat", "batch")),
        check_vma=False,
    )
```
